32 devices in a mesh: state: 4 (over z), tile: 8 (over y, x, core).
Axes of the slice: x: 2, y: 2, z: 4, core: 2. Of those that a mesh axis runs over, the one named last changes fastest.
Arguments:
- bands: bfloat16 [4, 240, 131072], P('state', None, 'tile')
- block_slot: int32 [4, 1024], P('state', 'tile'), may hold values from 0 to 7
- tile_counties: int32 [4, 64], P('state', 'tile'), may hold values from 0 to 95, as said below
- county_place: int32 [4, 96], P('state'), may hold values from 0 to 95, as said below
- label: int32 [4, 96], P('state', 'tile'), may hold values from -200 to 200
- w_first: bfloat16 [64, 240], replicated, may hold values from -0.375 to 0.375
- taps: float32 [3, 64], replicated, may hold values from -2 to 2
- w_second: bfloat16 [128, 64], replicated, may hold values from -0.75 to 0.75
- w_third: bfloat16 [128, 128], replicated, may hold values from -0.5 to 0.5
- w_head: bfloat16 [128], replicated, may hold values from -0.5 to 0.5
Outputs:
- county_mean: float32 [4, 96], P('state', 'tile')
- weight_grads: float32 [40256], replicated
The draws below stay inside these ranges and needn't reach their ends.
Inputs may be any that keep to these rules, and one draw needn't show every extreme that they name: `county_place`: each row is an ordering of the counties of one state region; the county at place p is owned by tile index p // 12 of that region. `tile_counties`: tile t's list names counties of its own state region owned by tile indices t, t + 1, ..., t + 4 - 1 (mod the tile axis's size); at most 4 entries of a list are owned by one tile index, and exactly 4 by t itself.
All inputs are finite; a program needn't handle non-finite values.
Results may differ from the reference program's by a relative error of at most 0.00064.
Values sent between devices are 32-bit elements; how exact they have to be, the bound alone decides.
A program may use at most 128 MiB of HBM per device.

```python
import jax
import jax.numpy as jnp
from jax import lax

FEAT = 240
C1 = 64
C2 = 128
ROW = 128
BLK_DEV = 128
CTY_DEV = 12
SLOTS = 8
MOST = 4
REACH = 4
PIX_DEV = 16384
COUNTIES = 96
GRADS = 40256
N_STATE = 4
N_TILE = 8


def place_table(key):
    keys = jax.random.split(jax.random.fold_in(key, 11), N_STATE)
    return jax.vmap(lambda one: jax.random.permutation(one, COUNTIES))(keys).astype(jnp.int32)


def draw_county_place(key, part):
    return place_table(key)


def draw_tile_counties(key, part):
    table = place_table(key)
    inverse = jnp.argsort(table, axis=1).astype(jnp.int32)
    first, second, third = jax.random.split(jax.random.fold_in(key, 23), 3)
    far = jax.random.randint(first, (N_STATE, N_TILE, SLOTS - MOST), 1, REACH).astype(jnp.int32)
    offsets = jnp.concatenate([jnp.zeros((N_STATE, N_TILE, MOST), jnp.int32), far], axis=2)
    orders = jax.vmap(lambda one: jax.random.permutation(one, SLOTS))(jax.random.split(second, N_STATE * N_TILE))
    offsets = jnp.take_along_axis(offsets, orders.reshape(N_STATE, N_TILE, SLOTS).astype(jnp.int32), axis=2)
    same = offsets[..., :, None] == offsets[..., None, :]
    before = jnp.arange(SLOTS)[None, :] < jnp.arange(SLOTS)[:, None]
    rank = jnp.sum(same & before, axis=-1).astype(jnp.int32)
    starts = jax.random.randint(third, (N_STATE, N_TILE, REACH), 0, CTY_DEV).astype(jnp.int32)
    start = jnp.take_along_axis(starts, offsets, axis=2)
    owner = (jnp.arange(N_TILE, dtype=jnp.int32)[None, :, None] + offsets) % N_TILE
    place = owner * CTY_DEV + (start + rank) % CTY_DEV
    county = jnp.take_along_axis(inverse, place.reshape(N_STATE, N_TILE * SLOTS), axis=1)
    return county.astype(jnp.int32)


def draw_bands(key, part):
    first, second = jax.random.split(jax.random.fold_in(key, 31), 2)
    blocks = N_TILE * BLK_DEV
    base = jax.random.normal(first, (N_STATE, FEAT, blocks, 1), jnp.float32)
    noise = jax.random.normal(second, (N_STATE, FEAT, blocks, ROW), jnp.float32)
    values = 0.8 * base + 0.6 * noise
    return values.reshape(N_STATE, FEAT, blocks * ROW).astype(jnp.bfloat16)


def touch_ends(entries, rng, low, largest):
    shape = entries.shape
    index_at = [jax.random.randint(jax.random.fold_in(rng, axis), (), 0, shape[axis]) for axis in range(len(shape))]
    entries = entries.at[tuple(index_at)].set(low)
    longest = shape.index(max(shape))
    index_at[longest] = (index_at[longest] + 1) % shape[longest]
    return entries.at[tuple(index_at)].set(largest)


def centred(stream_key, dims, scale, most, kind=jnp.bfloat16):
    entries = scale * jax.random.normal(stream_key, dims, jnp.float32)
    return jnp.clip(entries, min=-most, max=most).astype(kind)


def setup_inputs(seed: int = 0) -> dict:
    key_of = jax.random.split(jax.random.key(seed), 11)
    bands = draw_bands(jax.random.fold_in(key_of[10], 71), 0)
    block_slot = touch_ends(jax.random.randint(key_of[1], (N_STATE, N_TILE * BLK_DEV), 0, SLOTS), jax.random.fold_in(key_of[1], 1), 0, SLOTS - 1).astype(jnp.int32)
    tile_counties = draw_tile_counties(jax.random.fold_in(key_of[10], 71), 0)
    county_place = draw_county_place(jax.random.fold_in(key_of[10], 71), 0)
    label = touch_ends(jax.random.randint(key_of[4], (N_STATE, COUNTIES), -200, 201), jax.random.fold_in(key_of[4], 1), -200, 200).astype(jnp.int32)
    w_first = centred(key_of[5], (C1, FEAT), FEAT ** -0.5, 0.375)
    taps = centred(key_of[6], (3, C1), 0.5, 2.0, jnp.float32)
    w_second = centred(key_of[7], (C2, C1), C1 ** -0.5, 0.75)
    w_third = centred(key_of[8], (C2, C2), C2 ** -0.5, 0.5)
    w_head = centred(key_of[9], (C2,), C2 ** -0.5, 0.5)
    return {"bands": bands, "block_slot": block_slot, "tile_counties": tile_counties, "county_place": county_place, "label": label, "w_first": w_first, "taps": taps, "w_second": w_second, "w_third": w_third, "w_head": w_head}


def silu_parts(value):
    sig = jax.nn.sigmoid(value)
    return value * sig, sig * (1.0 + value * (1.0 - sig))


def along_rows(field, weights, row_len):
    chans, count = field.shape
    grid = field.reshape(chans, count // row_len, row_len)
    padded = jnp.pad(grid, ((0, 0), (0, 0), (1, 1)))
    out = weights[0][:, None, None] * padded[:, :, :-2] + weights[1][:, None, None] * grid + weights[2][:, None, None] * padded[:, :, 2:]
    return out.reshape(chans, count)


def tap_grads(field, upstream, row_len):
    chans, count = field.shape
    grid = field.reshape(chans, count // row_len, row_len)
    padded = jnp.pad(grid, ((0, 0), (0, 0), (1, 1)))
    above = upstream.reshape(grid.shape)
    return jnp.stack([jnp.sum(above * padded[:, :, :-2], axis=(1, 2)), jnp.sum(above * grid, axis=(1, 2)), jnp.sum(above * padded[:, :, 2:], axis=(1, 2))])


def contract_last(left, right):
    return lax.dot_general(left, right, (((1,), (1,)), ((), ())), preferred_element_type=jnp.float32)


def contract_first(left, right):
    return lax.dot_general(left, right, (((0,), (0,)), ((), ())), preferred_element_type=jnp.float32)


def forward(pixels, w_first, taps, w_second, w_third, w_head, row_len):
    h_one = jnp.dot(w_first, pixels, preferred_element_type=jnp.float32)
    s_one = along_rows(h_one, taps, row_len)
    a_one = silu_parts(s_one)[0].astype(jnp.bfloat16)
    h_two = jnp.dot(w_second, a_one, preferred_element_type=jnp.float32)
    a_two = silu_parts(h_two)[0].astype(jnp.bfloat16)
    h_three = jnp.dot(w_third, a_two, preferred_element_type=jnp.float32)
    a_three = (silu_parts(h_three)[0] + a_two.astype(jnp.float32)).astype(jnp.bfloat16)
    yhat = jnp.dot(w_head, a_three, preferred_element_type=jnp.float32)
    return h_one, s_one, a_one, h_two, a_two, h_three, a_three, yhat


def backward(pixels, saved, w_first, taps, w_second, w_third, w_head, cotangent, row_len):
    h_one, s_one, a_one, h_two, a_two, h_three, a_three, yhat = saved
    grad_in = cotangent.astype(jnp.bfloat16)
    d_head = jnp.dot(a_three, grad_in, preferred_element_type=jnp.float32)
    d_a3 = w_head.astype(jnp.float32)[:, None] * grad_in.astype(jnp.float32)[None, :]
    d_h3 = (d_a3 * silu_parts(h_three)[1]).astype(jnp.bfloat16)
    d_third = contract_last(d_h3, a_two)
    d_a2 = contract_first(w_third, d_h3) + d_a3
    d_h2 = (d_a2 * silu_parts(h_two)[1]).astype(jnp.bfloat16)
    d_second = contract_last(d_h2, a_one)
    d_a1 = contract_first(w_second, d_h2)
    d_s1 = d_a1 * silu_parts(s_one)[1]
    d_taps = tap_grads(h_one, d_s1, row_len)
    d_h1 = along_rows(d_s1, jnp.stack([taps[2], taps[1], taps[0]]), row_len).astype(jnp.bfloat16)
    d_first = contract_last(d_h1, pixels)
    return jnp.concatenate([d_first.reshape(-1), d_taps.reshape(-1), d_second.reshape(-1), d_third.reshape(-1), d_head])


def slot_stats(yhat, slots, slot_count):
    blocks = slots.shape[0]
    row_len = yhat.shape[0] // blocks
    member = (slots[None, :] == jnp.arange(slot_count, dtype=jnp.int32)[:, None]).astype(jnp.float32)
    block_sums = jnp.sum(yhat.reshape(blocks, row_len), axis=1)
    return jnp.sum(member * block_sums[None, :], axis=1), jnp.sum(member, axis=1) * row_len, member


def place_of(counties, table):
    hits = counties[:, None] == jnp.arange(table.shape[0], dtype=jnp.int32)[None, :]
    return jnp.sum(jnp.where(hits, table[None, :], 0), axis=1).astype(jnp.int32)


def judge(sums, counts, labels, devices):
    denom = jnp.maximum(counts, 1.0)
    mean = sums / denom
    live = (counts > 0.5).astype(jnp.float32)
    target = labels.astype(jnp.float32) * 0.01
    return mean, live * 2.0 * (mean - target) / (devices * denom)


def pixel_cotangent(member, slot_adjoint, row_len):
    block_adjoint = jnp.sum(member * slot_adjoint[:, None], axis=0)
    return jnp.broadcast_to(block_adjoint[:, None], (block_adjoint.shape[0], row_len)).reshape(-1)


def reference(bands, block_slot, tile_counties, county_place, label, w_first, taps, w_second, w_third, w_head):
    n_dev = N_STATE * N_TILE
    county_iota = jnp.arange(COUNTIES, dtype=jnp.int32)
    state_iota = jnp.arange(N_STATE, dtype=jnp.int32)

    def device_slice(index):
        state = (index // N_TILE).astype(jnp.int32)
        tile = (index % N_TILE).astype(jnp.int32)
        zero = jnp.zeros((), jnp.int32)
        pixels = lax.dynamic_slice(bands, (state, zero, tile * PIX_DEV), (1, FEAT, PIX_DEV))[0]
        slots = lax.dynamic_slice(block_slot, (state, tile * BLK_DEV), (1, BLK_DEV))[0]
        counties = lax.dynamic_slice(tile_counties, (state, tile * SLOTS), (1, SLOTS))[0]
        table = lax.dynamic_slice(county_place, (state, zero), (1, COUNTIES))[0]
        return state, pixels, slots, counties, table

    def first_pass(carry, index):
        sums, counts = carry
        state, pixels, slots, counties, table = device_slice(index)
        yhat = forward(pixels, w_first, taps, w_second, w_third, w_head, ROW)[-1]
        slot_sums, slot_counts, member = slot_stats(yhat, slots, SLOTS)
        hit = (place_of(counties, table)[:, None] == county_iota[None, :]).astype(jnp.float32)
        row = (state_iota == state).astype(jnp.float32)[:, None]
        sums = sums + row * jnp.sum(hit * slot_sums[:, None], axis=0)[None, :]
        counts = counts + row * jnp.sum(hit * slot_counts[:, None], axis=0)[None, :]
        return (sums, counts), None

    zeros = jnp.zeros((N_STATE, COUNTIES), jnp.float32)
    (sums, counts), _ = lax.scan(first_pass, (zeros, zeros), jnp.arange(n_dev, dtype=jnp.int32))
    county_mean, adjoint = judge(sums, counts, label, float(n_dev))

    def second_pass(total, index):
        state, pixels, slots, counties, table = device_slice(index)
        saved = forward(pixels, w_first, taps, w_second, w_third, w_head, ROW)
        member = slot_stats(saved[-1], slots, SLOTS)[2]
        hit = (place_of(counties, table)[:, None] == county_iota[None, :]).astype(jnp.float32)
        row = jnp.sum((state_iota == state).astype(jnp.float32)[:, None] * adjoint, axis=0)
        slot_adjoint = jnp.sum(hit * row[None, :], axis=1)
        cotangent = pixel_cotangent(member, slot_adjoint, ROW)
        return total + backward(pixels, saved, w_first, taps, w_second, w_third, w_head, cotangent, ROW), None

    weight_grads, _ = lax.scan(second_pass, jnp.zeros((GRADS,), jnp.float32), jnp.arange(n_dev, dtype=jnp.int32))
    return county_mean, weight_grads
```

```python
import functools

import jax
import jax.numpy as jnp
from jax import lax
from jax.experimental import pallas as pl
from jax.experimental.pallas import tpu as pltpu
from jax.sharding import PartitionSpec as P

REACH = 4
LANES = 128
GROUP = 8
STEP_ROWS = 4
DMA_STEPS = 8
MESH = pl.DeviceIdType.MESH
F32 = jnp.float32
BF16 = jnp.bfloat16


def mm(left, right):
    return jnp.dot(left, right, preferred_element_type=F32)


def mm_last(left, right):
    return lax.dot_general(left, right, (((1,), (1,)), ((), ())), preferred_element_type=F32)


def iota(shape, dim):
    return lax.broadcasted_iota(jnp.int32, shape, dim)


def to_column(row, size):
    eye = iota((size, size), 0) == iota((size, size), 1)
    return jnp.sum(jnp.where(eye, row, 0.0), axis=1, keepdims=True)


def to_row(column, size):
    eye = iota((size, size), 0) == iota((size, size), 1)
    return jnp.sum(jnp.where(eye, column, 0.0), axis=0, keepdims=True)


def gate_parts(half):
    twice = jnp.tanh(half) + 1.0
    act = half * twice
    return act, twice + act * (2.0 - twice)


def kernel(
    n_tile, n_state, share,
    bands, slot_row, counties, table, label, w_first, taps, w_second, w_third, w_head,
    mean_out, grads_out,
    x_s, a1_s, a2_s, d1_s, d2_s, d3_s, slot_s, g_s, w2_s, w2t_s, w3_s, w3t_s, wh_s,
    acc_first, acc_second, acc_third, acc_head, first_lo, first_hi, second_s, third_s,
    flat, msg, msgs, parts, zparts, whole,
    x_sem, msg_send, msg_recv, part_send, part_recv, z_send, z_recv, all_send, all_recv,
):
    me = lax.axis_index("tile")
    my_state = lax.axis_index("state")
    c1, feat = w_first.shape
    c2 = w_second.shape[0]
    blocks = slot_row.shape[1]
    pixels = bands.shape[2]
    row_len = pixels // blocks
    cty_dev = label.shape[1]
    places = table.shape[1]
    slot_count = counties.shape[1]
    step_px = STEP_ROWS * row_len
    dma_px = pixels // DMA_STEPS
    steps_per_dma = dma_px // step_px

    def band_copy(k):
        cols = pl.ds(pl.multiple_of(k * dma_px, dma_px), dma_px)
        return pltpu.make_async_copy(bands.at[0, :, cols], x_s.at[:, cols], x_sem.at[k])

    for k in range(DMA_STEPS):
        band_copy(k).start()

    def tile_peer(by):
        return lax.rem(me + by + n_tile, n_tile)

    def state_peer(by):
        return lax.rem(my_state + by + n_state, n_state)

    barrier = pltpu.get_barrier_semaphore()
    for by in range(1, n_tile):
        pl.semaphore_signal(barrier, inc=1, device_id={"tile": tile_peer(by)}, device_id_type=MESH)
    for by in range(1, n_state):
        pl.semaphore_signal(
            barrier, inc=1, device_id={"state": state_peer(by)}, device_id_type=MESH
        )

    slots = slot_row[...].astype(F32)
    slot_s[...] = jnp.broadcast_to(to_column(slots, blocks), (blocks, LANES))
    half_second = w_second[...].astype(F32) * 0.5
    half_third = w_third[...].astype(F32) * 0.5
    w2_s[...] = half_second.astype(BF16)
    w3_s[...] = half_third.astype(BF16)
    w2t_s[...] = half_second.T.astype(BF16)
    w3t_s[...] = half_third.T.astype(BF16)
    head_row = w_head[...].astype(F32)
    wh_s[...] = jnp.broadcast_to(to_column(head_row, c2) * 0.5, (c2, LANES))
    tap_cols = [to_column(taps[k : k + 1, :], c1) for k in range(3)]
    lane = iota((c1, LANES), 1)
    tap_prev = jnp.where(lane == 0, 0.0, tap_cols[0] * 0.5)
    tap_here = jnp.broadcast_to(tap_cols[1] * 0.5, (c1, LANES))
    tap_next = jnp.where(lane == LANES - 1, 0.0, tap_cols[2] * 0.5)
    acc_first[...] = jnp.zeros_like(acc_first)
    acc_second[...] = jnp.zeros_like(acc_second)
    acc_third[...] = jnp.zeros_like(acc_third)
    acc_head[...] = jnp.zeros_like(acc_head)
    slot_ids = iota((2 * GROUP, LANES), 0).astype(F32)

    def row_cols(j):
        return slice(j * row_len, (j + 1) * row_len)

    def forward(step):
        cols = pl.ds(pl.multiple_of(step * step_px, step_px), step_px)
        h1 = mm(w_first[...], x_s[:, cols])
        s1 = []
        for j in range(STEP_ROWS):
            h = h1[:, row_cols(j)]
            s1.append(
                tap_prev * pltpu.roll(h, 1, 1)
                + tap_here * h
                + tap_next * pltpu.roll(h, LANES - 1, 1)
            )
        a1, d1 = gate_parts(jnp.concatenate(s1, axis=1))
        d1_s[:, cols] = d1
        a1 = a1.astype(BF16)
        a1_s[:, cols] = a1
        a2, d2 = gate_parts(mm(w2_s[...], a1))
        d2_s[:, cols] = d2
        a2 = a2.astype(BF16)
        a2_s[:, cols] = a2
        a3, d3 = gate_parts(mm(w3_s[...], a2))
        d3_s[:, cols] = d3
        a3 = (a3 + a2.astype(F32)).astype(BF16)
        member = jnp.concatenate(
            [
                (slot_s[pl.ds(step * STEP_ROWS + j, 1), :] == slot_ids).astype(F32)
                for j in range(STEP_ROWS)
            ],
            axis=1,
        ).astype(BF16)
        acc_head[...] += mm_last(member, a3)

    def forward_dma(k, carry):
        band_copy(k).wait()

        def inner(i, c):
            forward(k * steps_per_dma + i)
            return c

        return lax.fori_loop(0, steps_per_dma, inner, carry)

    lax.fori_loop(0, DMA_STEPS, forward_dma, 0)

    head_sums = acc_head[0:GROUP, :]
    slot_sums = jnp.sum(head_sums * head_row, axis=1, keepdims=True)
    in_slot = (slots == slot_ids[0:GROUP, :]).astype(F32)
    slot_counts = jnp.sum(in_slot, axis=1, keepdims=True) * float(row_len)
    county = to_column(counties[...].astype(F32), slot_count)
    hits = county == iota((slot_count, places), 1).astype(F32)
    place = jnp.sum(jnp.where(hits, table[...].astype(F32), 0.0), axis=1, keepdims=True)
    place = place - (me * cty_dev).astype(F32)
    place = jnp.where(place < 0.0, place + float(places), place)
    pick = (place == iota((slot_count, LANES), 1).astype(F32)).astype(F32)
    msg[...] = jnp.zeros_like(msg)
    msg[0:1, :] = jnp.sum(pick * slot_sums, axis=0, keepdims=True)
    msg[1:2, :] = jnp.sum(pick * slot_counts, axis=0, keepdims=True)
    msg[2:3, 0:cty_dev] = label[...].astype(F32)

    pl.semaphore_wait(barrier, n_tile - 1 + n_state - 1)
    offsets = [by for by in range(1 - REACH, REACH) if by]
    copies = []
    for n, by in enumerate(offsets):
        copies.append(
            pltpu.make_async_remote_copy(
                src_ref=msg,
                dst_ref=msgs.at[n],
                send_sem=msg_send.at[n],
                recv_sem=msg_recv.at[n],
                device_id={"tile": tile_peer(by)},
                device_id_type=MESH,
            )
        )
        copies[-1].start()
    total = msg[...]
    for n, by in enumerate(offsets):
        copies[n].wait_recv()
        total = total + pltpu.roll(msgs[n], (-by * cty_dev) % LANES, 1)
    for copy in copies:
        copy.wait_send()
    sums, counts, target = total[0:1, :], total[1:2, :], total[2:3, :] * 0.01
    denom = jnp.maximum(counts, 1.0)
    mean = sums / denom
    mean_out[...] = mean[:, 0:cty_dev]
    adjoint = jnp.where(
        counts > 0.5, 2.0 * (mean - target) / (float(n_tile * n_state) * denom), 0.0
    )
    slot_g = jnp.sum(jnp.where(pick > 0.5, adjoint, 0.0), axis=1, keepdims=True)
    slot_g = slot_g.astype(BF16).astype(F32)
    all_slots = slot_s[...]
    g_rows = jnp.zeros((blocks, LANES), F32)
    for s in range(slot_count):
        g_rows = jnp.where(all_slots == float(s), slot_g[s : s + 1, 0:1], g_rows)
    g_s[...] = g_rows

    def backward(step, carry):
        cols = pl.ds(pl.multiple_of(step * step_px, step_px), step_px)
        x = x_s[:, cols]
        a1 = a1_s[:, cols]
        a2 = a2_s[:, cols]
        wh = wh_s[...]
        d_a3 = jnp.concatenate(
            [wh * g_s[pl.ds(step * STEP_ROWS + j, 1), :] for j in range(STEP_ROWS)], axis=1
        )
        d_h3 = (d_a3 * d3_s[:, cols]).astype(BF16)
        acc_third[...] += mm_last(d_h3, a2)
        d_h2 = ((mm(w3t_s[...], d_h3) + d_a3) * d2_s[:, cols]).astype(BF16)
        acc_second[...] += mm_last(d_h2, a1)
        d_s1 = mm(w2t_s[...], d_h2) * d1_s[:, cols]
        left, right = [], []
        for j in range(STEP_ROWS):
            d = d_s1[:, row_cols(j)]
            left.append(jnp.where(lane == LANES - 1, 0.0, pltpu.roll(d, LANES - 1, 1)))
            right.append(jnp.where(lane == 0, 0.0, pltpu.roll(d, 1, 1)))
        shifted = jnp.concatenate(
            [jnp.concatenate(left, axis=1), d_s1, jnp.concatenate(right, axis=1)], axis=0
        ).astype(BF16)
        acc_first[...] += mm_last(shifted, x)
        return carry

    lax.fori_loop(0, pixels // step_px, backward, 0)

    g_first = [acc_first[k * c1 : (k + 1) * c1, :] for k in range(3)]
    weights = w_first[...].astype(F32)
    d_first = tap_cols[0] * g_first[0] + tap_cols[1] * g_first[1] + tap_cols[2] * g_first[2]
    tap_rows = [
        to_row(jnp.sum(weights * g, axis=1, keepdims=True), c1) for g in g_first
    ]
    d_head = jnp.sum(head_sums * slot_g, axis=0, keepdims=True)
    first_lo[...] = d_first[:, 0:LANES]
    first_hi[:, 0 : feat - LANES] = d_first[:, LANES:feat]
    flat[...] = jnp.zeros_like(flat)
    period = feat * GROUP // LANES
    groups = c1 // GROUP
    at = iota((groups, LANES), 1)
    for j in range(period):
        chan, off = divmod(j * LANES, feat)
        lo = first_lo[pl.ds(chan, groups, stride=GROUP), :]
        hi = first_hi[pl.ds(chan, groups, stride=GROUP), :]
        value = pltpu.roll(hi, (-off) % LANES, 1)
        if off < LANES:
            lo_part = pltpu.roll(lo, (-off) % LANES, 1) if off else lo
            value = jnp.where(at < LANES - off, lo_part, value)
        if off + LANES > feat:
            after = first_lo[pl.ds(chan + 1, groups, stride=GROUP), :]
            value = jnp.where(at < feat - off, value, pltpu.roll(after, (feat - off) % LANES, 1))
        flat[pl.ds(j, groups, stride=period), :] = value
    base = c1 * feat // LANES
    half = LANES // 2
    second_s[...] = jnp.zeros_like(second_s)
    second_s[0:c2, 0:half] = acc_second[...]
    third_s[0:c2, :] = acc_third[...]
    third_s[c2 : c2 + 1, :] = d_head
    second_s[c2 : c2 + 1, :] = third_s[0:1, :]
    one = iota((1, LANES), 1) < half
    flat[base : base + 1, :] = jnp.concatenate(tap_rows[0:2], axis=1)
    flat[base + 1 : base + 2, :] = jnp.where(
        one,
        jnp.concatenate([tap_rows[2], tap_rows[2]], axis=1),
        pltpu.roll(second_s[0:1, :], half, 1),
    )
    odd = second_s[pl.ds(1, c2 // 2, stride=2), :]
    even = second_s[pl.ds(2, c2 // 2, stride=2), :]
    low = iota((c2 // 2, LANES), 1) < half
    flat[base + 2 : base + 2 + c2 // 2, :] = jnp.where(low, odd, pltpu.roll(even, half, 1))
    start = base + 2 + c2 // 2
    low = iota((c2, LANES), 1) < half
    flat[start : start + c2, :] = jnp.where(
        low, pltpu.roll(third_s[0:c2, :], half, 1), pltpu.roll(third_s[1 : c2 + 1, :], half, 1)
    )
    flat[start + c2 : start + c2 + 1, :] = jnp.where(one, pltpu.roll(d_head, half, 1), 0.0)

    def share_of(index):
        return pl.ds(pl.multiple_of(index * share, share), share)

    copies = []
    for by in range(1, n_tile):
        peer = tile_peer(by)
        copies.append(
            pltpu.make_async_remote_copy(
                src_ref=flat.at[share_of(peer)],
                dst_ref=parts.at[by - 1],
                send_sem=part_send.at[by - 1],
                recv_sem=part_recv.at[by - 1],
                device_id={"tile": peer},
                device_id_type=MESH,
            )
        )
        copies[-1].start()
    piece = flat[share_of(me), :]
    for n, copy in enumerate(copies):
        copy.wait_recv()
        piece = piece + parts[n]
    zparts[my_state] = piece
    zcopies = []
    for by in range(1, n_state):
        zcopies.append(
            pltpu.make_async_remote_copy(
                src_ref=zparts.at[my_state],
                dst_ref=zparts.at[my_state],
                send_sem=z_send.at[by - 1],
                recv_sem=z_recv.at[by - 1],
                device_id={"state": state_peer(by)},
                device_id_type=MESH,
            )
        )
        zcopies[-1].start()
    for copy in zcopies:
        copy.wait_recv()
    piece = zparts[0]
    for s in range(1, n_state):
        piece = piece + zparts[s]
    whole[share_of(me), :] = piece
    acopies = []
    for by in range(1, n_tile):
        acopies.append(
            pltpu.make_async_remote_copy(
                src_ref=whole.at[share_of(me)],
                dst_ref=whole.at[share_of(me)],
                send_sem=all_send.at[by - 1],
                recv_sem=all_recv.at[by - 1],
                device_id={"tile": tile_peer(by)},
                device_id_type=MESH,
            )
        )
        acopies[-1].start()
    for copy in copies:
        copy.wait_send()
    for copy in zcopies:
        copy.wait_send()
    for copy in acopies:
        copy.wait_recv()
    for copy in acopies:
        copy.wait_send()
    grads_out[...] = whole[...]


def on_device(
    n_tile, n_state,
    bands, block_slot, tile_counties, county_place, label, w_first, taps, w_second, w_third, w_head,
):
    feat, pixels = bands.shape[1:]
    c1, c2 = w_first.shape[0], w_second.shape[0]
    blocks = block_slot.shape[1]
    grads = c1 * feat + 3 * c1 + c2 * c1 + c2 * c2 + c2
    rows = pl.cdiv(grads, LANES)
    share = pl.cdiv(rows, n_tile * GROUP) * GROUP
    vmem = pl.BlockSpec(memory_space=pltpu.VMEM)
    dma = pltpu.SemaphoreType.DMA
    near = 2 * (REACH - 1)
    mean, out = pl.pallas_call(
        functools.partial(kernel, n_tile, n_state, share),
        out_shape=(
            jax.ShapeDtypeStruct(label.shape, F32),
            jax.ShapeDtypeStruct((n_tile * share, LANES), F32),
        ),
        in_specs=[pl.BlockSpec(memory_space=pl.ANY)] + [vmem] * 9,
        out_specs=(vmem, vmem),
        scratch_shapes=[
            pltpu.VMEM((feat, pixels), BF16),
            pltpu.VMEM((c1, pixels), BF16),
            pltpu.VMEM((c2, pixels), BF16),
            pltpu.VMEM((c1, pixels), F32),
            pltpu.VMEM((c2, pixels), F32),
            pltpu.VMEM((c2, pixels), F32),
            pltpu.VMEM((blocks, LANES), F32),
            pltpu.VMEM((blocks, LANES), F32),
            pltpu.VMEM((c2, c1), BF16),
            pltpu.VMEM((c1, c2), BF16),
            pltpu.VMEM((c2, c2), BF16),
            pltpu.VMEM((c2, c2), BF16),
            pltpu.VMEM((c2, LANES), F32),
            pltpu.VMEM((3 * c1, feat), F32),
            pltpu.VMEM((c2, c1), F32),
            pltpu.VMEM((c2, c2), F32),
            pltpu.VMEM((2 * GROUP, c2), F32),
            pltpu.VMEM((c1, LANES), F32),
            pltpu.VMEM((c1, LANES), F32),
            pltpu.VMEM((c2 + GROUP, LANES), F32),
            pltpu.VMEM((c2 + GROUP, LANES), F32),
            pltpu.VMEM((n_tile * share, LANES), F32),
            pltpu.VMEM((GROUP, LANES), F32),
            pltpu.VMEM((near, GROUP, LANES), F32),
            pltpu.VMEM((n_tile - 1, share, LANES), F32),
            pltpu.VMEM((n_state, share, LANES), F32),
            pltpu.VMEM((n_tile * share, LANES), F32),
            dma((DMA_STEPS,)),
            dma((near,)),
            dma((near,)),
            dma((n_tile - 1,)),
            dma((n_tile - 1,)),
            dma((n_state - 1,)),
            dma((n_state - 1,)),
            dma((n_tile - 1,)),
            dma((n_tile - 1,)),
        ],
        compiler_params=pltpu.CompilerParams(
            collective_id=0, has_side_effects=True, vmem_limit_bytes=56 * 2**20
        ),
    )(
        bands, block_slot, tile_counties, county_place, label,
        w_first, taps, w_second, w_third, w_head.reshape(1, -1),
    )
    return mean, out.reshape(-1)[:grads]


def solution(mesh):
    in_specs = (
        P("state", None, "tile"),
        P("state", "tile"),
        P("state", "tile"),
        P("state", None),
        P("state", "tile"),
        P(),
        P(),
        P(),
        P(),
        P(),
    )
    return jax.shard_map(
        functools.partial(on_device, mesh.shape["tile"], mesh.shape["state"]),
        mesh=mesh,
        in_specs=in_specs,
        out_specs=(P("state", "tile"), P()),
        check_vma=False,
    )
```

```python
import functools

import jax
import jax.numpy as jnp
from jax import lax
from jax.experimental import pallas as pl
from jax.experimental.pallas import tpu as pltpu
from jax.sharding import PartitionSpec as P

REACH = 4
LANES = 128
GROUP = 8
STEP_ROWS = 8
DMA_STEPS = 8
MESH = pl.DeviceIdType.MESH
F32 = jnp.float32
BF16 = jnp.bfloat16


def mm(left, right):
    return jnp.dot(left, right, preferred_element_type=F32)


def mm_last(left, right):
    return lax.dot_general(left, right, (((1,), (1,)), ((), ())), preferred_element_type=F32)


def iota(shape, dim):
    return lax.broadcasted_iota(jnp.int32, shape, dim)


def to_column(row, size):
    eye = iota((size, size), 0) == iota((size, size), 1)
    return jnp.sum(jnp.where(eye, row, 0.0), axis=1, keepdims=True)


def to_row(column, size):
    eye = iota((size, size), 0) == iota((size, size), 1)
    return jnp.sum(jnp.where(eye, column, 0.0), axis=0, keepdims=True)


def gate_parts(half):
    twice = jnp.tanh(half) + 1.0
    act = half * twice
    return act, twice + act * (2.0 - twice)


def kernel(
    n_tile, n_state, share,
    bands, slot_row, counties, table, label, w_first, taps, w_second, w_third, w_head,
    mean_out, grads_out,
    x_s, a1_s, a2_s, d1_s, d2_s, d3_s, slot_s, g_s, w2_s, w2t_s, w3_s, w3t_s, wh_s,
    acc_first, acc_second, acc_third, acc_head, first_lo, first_hi, second_s, third_s,
    flat, msg, msgs, parts, zparts, whole,
    x_sem, msg_send, msg_recv, part_send, part_recv, z_send, z_recv, all_send, all_recv,
):
    me = lax.axis_index("tile")
    my_state = lax.axis_index("state")
    c1, feat = w_first.shape
    c2 = w_second.shape[1]
    blocks = slot_row.shape[1]
    pixels = bands.shape[2]
    row_len = pixels // blocks
    cty_dev = label.shape[1]
    places = table.shape[1]
    slot_count = counties.shape[1]
    step_px = STEP_ROWS * row_len
    dma_px = pixels // DMA_STEPS
    steps_per_dma = dma_px // step_px

    def band_copy(k):
        cols = pl.ds(pl.multiple_of(k * dma_px, dma_px), dma_px)
        return pltpu.make_async_copy(bands.at[0, :, cols], x_s.at[:, cols], x_sem.at[k])

    for k in range(DMA_STEPS):
        band_copy(k).start()

    def tile_peer(by):
        return lax.rem(me + by + n_tile, n_tile)

    def state_peer(by):
        return lax.rem(my_state + by + n_state, n_state)

    barrier = pltpu.get_barrier_semaphore()
    for by in range(1, n_tile):
        pl.semaphore_signal(barrier, inc=1, device_id={"tile": tile_peer(by)}, device_id_type=MESH)
    for by in range(1, n_state):
        pl.semaphore_signal(
            barrier, inc=1, device_id={"state": state_peer(by)}, device_id_type=MESH
        )

    slots = slot_row[...].astype(F32)
    slot_s[...] = jnp.broadcast_to(to_column(slots, blocks), (blocks, LANES))
    half_second = w_second[...].astype(F32) * 0.5
    half_third = w_third[...].astype(F32) * 0.5
    w2t_s[...] = half_second.astype(BF16)
    w3_s[...] = half_third.astype(BF16)
    w2_s[...] = half_second.T.astype(BF16)
    w3t_s[...] = half_third.T.astype(BF16)
    head_row = w_head[...].astype(F32)
    wh_s[...] = jnp.broadcast_to(to_column(head_row, c2) * 0.5, (c2, LANES))
    tap_cols = [to_column(taps[k : k + 1, :], c1) for k in range(3)]
    lane = iota((c1, LANES), 1)
    tap_prev = jnp.where(lane == 0, 0.0, tap_cols[0] * 0.5)
    tap_here = jnp.broadcast_to(tap_cols[1] * 0.5, (c1, LANES))
    tap_next = jnp.where(lane == LANES - 1, 0.0, tap_cols[2] * 0.5)
    acc_first[...] = jnp.zeros_like(acc_first)
    acc_second[...] = jnp.zeros_like(acc_second)
    acc_third[...] = jnp.zeros_like(acc_third)
    acc_head[...] = jnp.zeros_like(acc_head)
    slot_ids = iota((2 * GROUP, LANES), 0).astype(F32)

    def row_cols(j):
        return slice(j * row_len, (j + 1) * row_len)

    def forward(step):
        cols = pl.ds(pl.multiple_of(step * step_px, step_px), step_px)
        h1 = mm(w_first[...], x_s[:, cols])
        s1 = []
        for j in range(STEP_ROWS):
            h = h1[:, row_cols(j)]
            s1.append(
                tap_prev * pltpu.roll(h, 1, 1)
                + tap_here * h
                + tap_next * pltpu.roll(h, LANES - 1, 1)
            )
        a1, d1 = gate_parts(jnp.concatenate(s1, axis=1))
        d1_s[:, cols] = d1
        a1 = a1.astype(BF16)
        a1_s[:, cols] = a1
        a2, d2 = gate_parts(mm(w2_s[...], a1))
        d2_s[:, cols] = d2
        a2 = a2.astype(BF16)
        a2_s[:, cols] = a2
        a3, d3 = gate_parts(mm(w3_s[...], a2))
        d3_s[:, cols] = d3
        a3 = (a3 + a2.astype(F32)).astype(BF16)
        member = jnp.concatenate(
            [
                (slot_s[pl.ds(step * STEP_ROWS + j, 1), :] == slot_ids).astype(F32)
                for j in range(STEP_ROWS)
            ],
            axis=1,
        ).astype(BF16)
        acc_head[...] += mm_last(member, a3)

    def forward_dma(k, carry):
        band_copy(k).wait()

        def inner(i, c):
            forward(k * steps_per_dma + i)
            return c

        return lax.fori_loop(0, steps_per_dma, inner, carry)

    lax.fori_loop(0, DMA_STEPS, forward_dma, 0)

    head_sums = acc_head[0:GROUP, :]
    slot_sums = jnp.sum(head_sums * head_row, axis=1, keepdims=True)
    in_slot = (slots == slot_ids[0:GROUP, :]).astype(F32)
    slot_counts = jnp.sum(in_slot, axis=1, keepdims=True) * float(row_len)
    county = to_column(counties[...].astype(F32), slot_count)
    hits = county == iota((slot_count, places), 1).astype(F32)
    place = jnp.sum(jnp.where(hits, table[...].astype(F32), 0.0), axis=1, keepdims=True)
    place = place - (me * cty_dev).astype(F32)
    place = jnp.where(place < 0.0, place + float(places), place)
    pick = (place == iota((slot_count, LANES), 1).astype(F32)).astype(F32)
    msg[...] = jnp.zeros_like(msg)
    msg[0:1, :] = jnp.sum(pick * slot_sums, axis=0, keepdims=True)
    msg[1:2, :] = jnp.sum(pick * slot_counts, axis=0, keepdims=True)
    msg[2:3, 0:cty_dev] = label[...].astype(F32)

    pl.semaphore_wait(barrier, n_tile - 1 + n_state - 1)
    offsets = [by for by in range(1 - REACH, REACH) if by]
    copies = []
    for n, by in enumerate(offsets):
        copies.append(
            pltpu.make_async_remote_copy(
                src_ref=msg,
                dst_ref=msgs.at[n],
                send_sem=msg_send.at[n],
                recv_sem=msg_recv.at[n],
                device_id={"tile": tile_peer(by)},
                device_id_type=MESH,
            )
        )
        copies[-1].start()
    total = msg[...]
    for n, by in enumerate(offsets):
        copies[n].wait_recv()
        total = total + pltpu.roll(msgs[n], (-by * cty_dev) % LANES, 1)
    for copy in copies:
        copy.wait_send()
    sums, counts, target = total[0:1, :], total[1:2, :], total[2:3, :] * 0.01
    denom = jnp.maximum(counts, 1.0)
    mean = sums / denom
    mean_out[...] = mean[:, 0:cty_dev]
    adjoint = jnp.where(
        counts > 0.5, 2.0 * (mean - target) / (float(n_tile * n_state) * denom), 0.0
    )
    slot_g = jnp.sum(jnp.where(pick > 0.5, adjoint, 0.0), axis=1, keepdims=True)
    slot_g = slot_g.astype(BF16).astype(F32)
    all_slots = slot_s[...]
    g_rows = jnp.zeros((blocks, LANES), F32)
    for s in range(slot_count):
        g_rows = jnp.where(all_slots == float(s), slot_g[s : s + 1, 0:1], g_rows)
    g_s[...] = g_rows

    def backward(step, carry):
        cols = pl.ds(pl.multiple_of(step * step_px, step_px), step_px)
        x = x_s[:, cols]
        a1 = a1_s[:, cols]
        a2 = a2_s[:, cols]
        wh = wh_s[...]
        d_a3 = jnp.concatenate(
            [wh * g_s[pl.ds(step * STEP_ROWS + j, 1), :] for j in range(STEP_ROWS)], axis=1
        )
        d_h3 = (d_a3 * d3_s[:, cols]).astype(BF16)
        acc_third[...] += mm_last(d_h3, a2)
        d_h2 = ((mm(w3t_s[...], d_h3) + d_a3) * d2_s[:, cols]).astype(BF16)
        acc_second[...] += mm_last(d_h2, a1)
        d_s1 = mm(w2t_s[...], d_h2) * d1_s[:, cols]
        left, right = [], []
        for j in range(STEP_ROWS):
            d = d_s1[:, row_cols(j)]
            left.append(jnp.where(lane == LANES - 1, 0.0, pltpu.roll(d, LANES - 1, 1)))
            right.append(jnp.where(lane == 0, 0.0, pltpu.roll(d, 1, 1)))
        shifted = jnp.concatenate(
            [jnp.concatenate(left, axis=1), d_s1, jnp.concatenate(right, axis=1)], axis=0
        ).astype(BF16)
        acc_first[...] += mm_last(shifted, x)
        return carry

    lax.fori_loop(0, pixels // step_px, backward, 0)

    g_first = [acc_first[k * c1 : (k + 1) * c1, :] for k in range(3)]
    weights = w_first[...].astype(F32)
    d_first = tap_cols[0] * g_first[0] + tap_cols[1] * g_first[1] + tap_cols[2] * g_first[2]
    tap_rows = [
        to_row(jnp.sum(weights * g, axis=1, keepdims=True), c1) for g in g_first
    ]
    d_head = jnp.sum(head_sums * slot_g, axis=0, keepdims=True)
    first_lo[...] = d_first[:, 0:LANES]
    first_hi[:, 0 : feat - LANES] = d_first[:, LANES:feat]
    flat[...] = jnp.zeros_like(flat)
    period = feat * GROUP // LANES
    groups = c1 // GROUP
    at = iota((groups, LANES), 1)
    for j in range(period):
        chan, off = divmod(j * LANES, feat)
        lo = first_lo[pl.ds(chan, groups, stride=GROUP), :]
        hi = first_hi[pl.ds(chan, groups, stride=GROUP), :]
        value = pltpu.roll(hi, (-off) % LANES, 1)
        if off < LANES:
            lo_part = pltpu.roll(lo, (-off) % LANES, 1) if off else lo
            value = jnp.where(at < LANES - off, lo_part, value)
        if off + LANES > feat:
            after = first_lo[pl.ds(chan + 1, groups, stride=GROUP), :]
            value = jnp.where(at < feat - off, value, pltpu.roll(after, (feat - off) % LANES, 1))
        flat[pl.ds(j, groups, stride=period), :] = value
    base = c1 * feat // LANES
    half = LANES // 2
    second_s[...] = jnp.zeros_like(second_s)
    second_s[0:c2, 0:half] = acc_second[...]
    third_s[0:c2, :] = acc_third[...]
    third_s[c2 : c2 + 1, :] = d_head
    second_s[c2 : c2 + 1, :] = third_s[0:1, :]
    one = iota((1, LANES), 1) < half
    flat[base : base + 1, :] = jnp.concatenate(tap_rows[0:2], axis=1)
    flat[base + 1 : base + 2, :] = jnp.where(
        one,
        jnp.concatenate([tap_rows[2], tap_rows[2]], axis=1),
        pltpu.roll(second_s[0:1, :], half, 1),
    )
    odd = second_s[pl.ds(1, c2 // 2, stride=2), :]
    even = second_s[pl.ds(2, c2 // 2, stride=2), :]
    low = iota((c2 // 2, LANES), 1) < half
    flat[base + 2 : base + 2 + c2 // 2, :] = jnp.where(low, odd, pltpu.roll(even, half, 1))
    start = base + 2 + c2 // 2
    low = iota((c2, LANES), 1) < half
    flat[start : start + c2, :] = jnp.where(
        low, pltpu.roll(third_s[0:c2, :], half, 1), pltpu.roll(third_s[1 : c2 + 1, :], half, 1)
    )
    flat[start + c2 : start + c2 + 1, :] = jnp.where(one, pltpu.roll(d_head, half, 1), 0.0)

    def share_of(index):
        return pl.ds(pl.multiple_of(index * share, share), share)

    copies = []
    for by in range(1, n_tile):
        peer = tile_peer(by)
        copies.append(
            pltpu.make_async_remote_copy(
                src_ref=flat.at[share_of(peer)],
                dst_ref=parts.at[by - 1],
                send_sem=part_send.at[by - 1],
                recv_sem=part_recv.at[by - 1],
                device_id={"tile": peer},
                device_id_type=MESH,
            )
        )
        copies[-1].start()
    piece = flat[share_of(me), :]
    for n, copy in enumerate(copies):
        copy.wait_recv()
        piece = piece + parts[n]
    zparts[my_state] = piece
    zcopies = []
    for by in range(1, n_state):
        zcopies.append(
            pltpu.make_async_remote_copy(
                src_ref=zparts.at[my_state],
                dst_ref=zparts.at[my_state],
                send_sem=z_send.at[by - 1],
                recv_sem=z_recv.at[by - 1],
                device_id={"state": state_peer(by)},
                device_id_type=MESH,
            )
        )
        zcopies[-1].start()
    for copy in zcopies:
        copy.wait_recv()
    piece = zparts[0]
    for s in range(1, n_state):
        piece = piece + zparts[s]
    whole[share_of(me), :] = piece
    acopies = []
    for by in range(1, n_tile):
        acopies.append(
            pltpu.make_async_remote_copy(
                src_ref=whole.at[share_of(me)],
                dst_ref=whole.at[share_of(me)],
                send_sem=all_send.at[by - 1],
                recv_sem=all_recv.at[by - 1],
                device_id={"tile": tile_peer(by)},
                device_id_type=MESH,
            )
        )
        acopies[-1].start()
    for copy in copies:
        copy.wait_send()
    for copy in zcopies:
        copy.wait_send()
    for copy in acopies:
        copy.wait_recv()
    for copy in acopies:
        copy.wait_send()
    grads_out[...] = whole[...]


def on_device(
    n_tile, n_state,
    bands, block_slot, tile_counties, county_place, label, w_first, taps, w_second, w_third, w_head,
):
    feat, pixels = bands.shape[1:]
    c1, c2 = w_first.shape[0], w_second.shape[0]
    blocks = block_slot.shape[1]
    grads = c1 * feat + 3 * c1 + c2 * c1 + c2 * c2 + c2
    rows = pl.cdiv(grads, LANES)
    share = pl.cdiv(rows, n_tile * GROUP) * GROUP
    vmem = pl.BlockSpec(memory_space=pltpu.VMEM)
    dma = pltpu.SemaphoreType.DMA
    near = 2 * (REACH - 1)
    mean, out = pl.pallas_call(
        functools.partial(kernel, n_tile, n_state, share),
        out_shape=(
            jax.ShapeDtypeStruct(label.shape, F32),
            jax.ShapeDtypeStruct((n_tile * share, LANES), F32),
        ),
        in_specs=[pl.BlockSpec(memory_space=pl.ANY)] + [vmem] * 9,
        out_specs=(vmem, vmem),
        scratch_shapes=[
            pltpu.VMEM((feat, pixels), BF16),
            pltpu.VMEM((c1, pixels), BF16),
            pltpu.VMEM((c2, pixels), BF16),
            pltpu.VMEM((c1, pixels), F32),
            pltpu.VMEM((c2, pixels), F32),
            pltpu.VMEM((c2, pixels), F32),
            pltpu.VMEM((blocks, LANES), F32),
            pltpu.VMEM((blocks, LANES), F32),
            pltpu.VMEM((c2, c1), BF16),
            pltpu.VMEM((c1, c2), BF16),
            pltpu.VMEM((c2, c2), BF16),
            pltpu.VMEM((c2, c2), BF16),
            pltpu.VMEM((c2, LANES), F32),
            pltpu.VMEM((3 * c1, feat), F32),
            pltpu.VMEM((c2, c1), F32),
            pltpu.VMEM((c2, c2), F32),
            pltpu.VMEM((2 * GROUP, c2), F32),
            pltpu.VMEM((c1, LANES), F32),
            pltpu.VMEM((c1, LANES), F32),
            pltpu.VMEM((c2 + GROUP, LANES), F32),
            pltpu.VMEM((c2 + GROUP, LANES), F32),
            pltpu.VMEM((n_tile * share, LANES), F32),
            pltpu.VMEM((GROUP, LANES), F32),
            pltpu.VMEM((near, GROUP, LANES), F32),
            pltpu.VMEM((n_tile - 1, share, LANES), F32),
            pltpu.VMEM((n_state, share, LANES), F32),
            pltpu.VMEM((n_tile * share, LANES), F32),
            dma((DMA_STEPS,)),
            dma((near,)),
            dma((near,)),
            dma((n_tile - 1,)),
            dma((n_tile - 1,)),
            dma((n_state - 1,)),
            dma((n_state - 1,)),
            dma((n_tile - 1,)),
            dma((n_tile - 1,)),
        ],
        compiler_params=pltpu.CompilerParams(
            collective_id=0, has_side_effects=True, vmem_limit_bytes=56 * 2**20
        ),
    )(
        bands, block_slot, tile_counties, county_place, label,
        w_first, taps, w_second.T, w_third, w_head.reshape(1, -1),
    )
    return mean, out.reshape(-1)[:grads]


def solution(mesh):
    in_specs = (
        P("state", None, "tile"),
        P("state", "tile"),
        P("state", "tile"),
        P("state", None),
        P("state", "tile"),
        P(),
        P(),
        P(),
        P(),
        P(),
    )
    return jax.shard_map(
        functools.partial(on_device, mesh.shape["tile"], mesh.shape["state"]),
        mesh=mesh,
        in_specs=in_specs,
        out_specs=(P("state", "tile"), P()),
        check_vma=False,
    )
```

```python
import functools

import jax
import jax.numpy as jnp
from jax import lax
from jax.experimental import pallas as pl
from jax.experimental.pallas import tpu as pltpu
from jax.sharding import PartitionSpec as P

REACH = 4
LANES = 128
GROUP = 8
STEP_ROWS = 16
DMA_STEPS = 8
MESH = pl.DeviceIdType.MESH
F32 = jnp.float32
BF16 = jnp.bfloat16


def mm(left, right):
    return jnp.dot(left, right, preferred_element_type=F32)


def mm_last(left, right):
    return lax.dot_general(left, right, (((1,), (1,)), ((), ())), preferred_element_type=F32)


def iota(shape, dim):
    return lax.broadcasted_iota(jnp.int32, shape, dim)


def to_column(row, size):
    eye = iota((size, size), 0) == iota((size, size), 1)
    return jnp.sum(jnp.where(eye, row, 0.0), axis=1, keepdims=True)


def to_row(column, size):
    eye = iota((size, size), 0) == iota((size, size), 1)
    return jnp.sum(jnp.where(eye, column, 0.0), axis=0, keepdims=True)


def gate_parts(half):
    twice = jnp.tanh(half) + 1.0
    act = half * twice
    return act, twice + act * (2.0 - twice)


def kernel(
    n_tile, n_state, share,
    bands, slot_row, counties, table, label, w_first, taps, w_second, w_third, w_head,
    mean_out, grads_out,
    x_s, a1_s, a2_s, d1_s, d2_s, d3_s, slot_s, g_s, w2_s, w2t_s, w3_s, w3t_s, wh_s,
    acc_first, acc_second, acc_third, acc_head, first_lo, first_hi, second_s, third_s,
    flat, msg, msgs, parts, zparts, whole,
    x_sem, msg_send, msg_recv, part_send, part_recv, z_send, z_recv, all_send, all_recv,
):
    me = lax.axis_index("tile")
    my_state = lax.axis_index("state")
    c1, feat = w_first.shape
    c2 = w_second.shape[1]
    blocks = slot_row.shape[1]
    pixels = bands.shape[2]
    row_len = pixels // blocks
    cty_dev = label.shape[1]
    places = table.shape[1]
    slot_count = counties.shape[1]
    step_px = STEP_ROWS * row_len
    dma_px = pixels // DMA_STEPS
    steps_per_dma = dma_px // step_px

    def band_copy(k):
        cols = pl.ds(pl.multiple_of(k * dma_px, dma_px), dma_px)
        return pltpu.make_async_copy(bands.at[0, :, cols], x_s.at[:, cols], x_sem.at[k])

    for k in range(DMA_STEPS):
        band_copy(k).start()

    def tile_peer(by):
        return lax.rem(me + by + n_tile, n_tile)

    def state_peer(by):
        return lax.rem(my_state + by + n_state, n_state)

    barrier = pltpu.get_barrier_semaphore()
    for by in range(1, n_tile):
        pl.semaphore_signal(barrier, inc=1, device_id={"tile": tile_peer(by)}, device_id_type=MESH)
    for by in range(1, n_state):
        pl.semaphore_signal(
            barrier, inc=1, device_id={"state": state_peer(by)}, device_id_type=MESH
        )

    slots = slot_row[...].astype(F32)
    slot_s[...] = jnp.broadcast_to(to_column(slots, blocks), (blocks, LANES))
    half_second = w_second[...].astype(F32) * 0.5
    half_third = w_third[...].astype(F32) * 0.5
    w2t_s[...] = half_second.astype(BF16)
    w3_s[...] = half_third.astype(BF16)
    w2_s[...] = half_second.T.astype(BF16)
    w3t_s[...] = half_third.T.astype(BF16)
    head_row = w_head[...].astype(F32)
    wh_s[...] = jnp.broadcast_to(to_column(head_row, c2) * 0.5, (c2, LANES))
    tap_cols = [to_column(taps[k : k + 1, :], c1) for k in range(3)]
    lane = iota((c1, LANES), 1)
    tap_prev = jnp.where(lane == 0, 0.0, tap_cols[0] * 0.5)
    tap_here = jnp.broadcast_to(tap_cols[1] * 0.5, (c1, LANES))
    tap_next = jnp.where(lane == LANES - 1, 0.0, tap_cols[2] * 0.5)
    acc_first[...] = jnp.zeros_like(acc_first)
    acc_second[...] = jnp.zeros_like(acc_second)
    acc_third[...] = jnp.zeros_like(acc_third)
    acc_head[...] = jnp.zeros_like(acc_head)
    slot_ids = iota((2 * GROUP, LANES), 0).astype(F32)

    def row_cols(j):
        return slice(j * row_len, (j + 1) * row_len)

    def forward(step):
        cols = pl.ds(pl.multiple_of(step * step_px, step_px), step_px)
        h1 = mm(w_first[...], x_s[:, cols])
        s1 = []
        for j in range(STEP_ROWS):
            h = h1[:, row_cols(j)]
            s1.append(
                tap_prev * pltpu.roll(h, 1, 1)
                + tap_here * h
                + tap_next * pltpu.roll(h, LANES - 1, 1)
            )
        a1, d1 = gate_parts(jnp.concatenate(s1, axis=1))
        d1_s[:, cols] = d1
        a1 = a1.astype(BF16)
        a1_s[:, cols] = a1
        a2, d2 = gate_parts(mm(w2_s[...], a1))
        d2_s[:, cols] = d2
        a2 = a2.astype(BF16)
        a2_s[:, cols] = a2
        a3, d3 = gate_parts(mm(w3_s[...], a2))
        d3_s[:, cols] = d3
        a3 = (a3 + a2.astype(F32)).astype(BF16)
        member = jnp.concatenate(
            [
                (slot_s[pl.ds(step * STEP_ROWS + j, 1), :] == slot_ids).astype(F32)
                for j in range(STEP_ROWS)
            ],
            axis=1,
        ).astype(BF16)
        acc_head[...] += mm_last(member, a3)

    def forward_dma(k, carry):
        band_copy(k).wait()

        def inner(i, c):
            forward(k * steps_per_dma + i)
            return c

        return lax.fori_loop(0, steps_per_dma, inner, carry)

    lax.fori_loop(0, DMA_STEPS, forward_dma, 0)

    head_sums = acc_head[0:GROUP, :]
    slot_sums = jnp.sum(head_sums * head_row, axis=1, keepdims=True)
    in_slot = (slots == slot_ids[0:GROUP, :]).astype(F32)
    slot_counts = jnp.sum(in_slot, axis=1, keepdims=True) * float(row_len)
    county = to_column(counties[...].astype(F32), slot_count)
    hits = county == iota((slot_count, places), 1).astype(F32)
    place = jnp.sum(jnp.where(hits, table[...].astype(F32), 0.0), axis=1, keepdims=True)
    place = place - (me * cty_dev).astype(F32)
    place = jnp.where(place < 0.0, place + float(places), place)
    pick = (place == iota((slot_count, LANES), 1).astype(F32)).astype(F32)
    msg[...] = jnp.zeros_like(msg)
    msg[0:1, :] = jnp.sum(pick * slot_sums, axis=0, keepdims=True)
    msg[1:2, :] = jnp.sum(pick * slot_counts, axis=0, keepdims=True)
    msg[2:3, 0:cty_dev] = label[...].astype(F32)

    pl.semaphore_wait(barrier, n_tile - 1 + n_state - 1)
    offsets = [by for by in range(1 - REACH, REACH) if by]
    copies = []
    for n, by in enumerate(offsets):
        copies.append(
            pltpu.make_async_remote_copy(
                src_ref=msg,
                dst_ref=msgs.at[n],
                send_sem=msg_send.at[n],
                recv_sem=msg_recv.at[n],
                device_id={"tile": tile_peer(by)},
                device_id_type=MESH,
            )
        )
        copies[-1].start()
    total = msg[...]
    for n, by in enumerate(offsets):
        copies[n].wait_recv()
        total = total + pltpu.roll(msgs[n], (-by * cty_dev) % LANES, 1)
    for copy in copies:
        copy.wait_send()
    sums, counts, target = total[0:1, :], total[1:2, :], total[2:3, :] * 0.01
    denom = jnp.maximum(counts, 1.0)
    mean = sums / denom
    mean_out[...] = mean[:, 0:cty_dev]
    adjoint = jnp.where(
        counts > 0.5, 2.0 * (mean - target) / (float(n_tile * n_state) * denom), 0.0
    )
    slot_g = jnp.sum(jnp.where(pick > 0.5, adjoint, 0.0), axis=1, keepdims=True)
    slot_g = slot_g.astype(BF16).astype(F32)
    all_slots = slot_s[...]
    g_rows = jnp.zeros((blocks, LANES), F32)
    for s in range(slot_count):
        g_rows = jnp.where(all_slots == float(s), slot_g[s : s + 1, 0:1], g_rows)
    g_s[...] = g_rows

    def backward(step, carry):
        cols = pl.ds(pl.multiple_of(step * step_px, step_px), step_px)
        x = x_s[:, cols]
        a1 = a1_s[:, cols]
        a2 = a2_s[:, cols]
        wh = wh_s[...]
        d_a3 = jnp.concatenate(
            [wh * g_s[pl.ds(step * STEP_ROWS + j, 1), :] for j in range(STEP_ROWS)], axis=1
        )
        d_h3 = (d_a3 * d3_s[:, cols]).astype(BF16)
        acc_third[...] += mm_last(d_h3, a2)
        d_h2 = ((mm(w3t_s[...], d_h3) + d_a3) * d2_s[:, cols]).astype(BF16)
        acc_second[...] += mm_last(d_h2, a1)
        d_s1 = mm(w2t_s[...], d_h2) * d1_s[:, cols]
        left, right = [], []
        for j in range(STEP_ROWS):
            d = d_s1[:, row_cols(j)]
            left.append(jnp.where(lane == LANES - 1, 0.0, pltpu.roll(d, LANES - 1, 1)))
            right.append(jnp.where(lane == 0, 0.0, pltpu.roll(d, 1, 1)))
        shifted = jnp.concatenate(
            [jnp.concatenate(left, axis=1), d_s1, jnp.concatenate(right, axis=1)], axis=0
        ).astype(BF16)
        acc_first[...] += mm_last(shifted, x)
        return carry

    lax.fori_loop(0, pixels // step_px, backward, 0)

    g_first = [acc_first[k * c1 : (k + 1) * c1, :] for k in range(3)]
    weights = w_first[...].astype(F32)
    d_first = tap_cols[0] * g_first[0] + tap_cols[1] * g_first[1] + tap_cols[2] * g_first[2]
    tap_rows = [
        to_row(jnp.sum(weights * g, axis=1, keepdims=True), c1) for g in g_first
    ]
    d_head = jnp.sum(head_sums * slot_g, axis=0, keepdims=True)
    first_lo[...] = d_first[:, 0:LANES]
    first_hi[:, 0 : feat - LANES] = d_first[:, LANES:feat]
    flat[...] = jnp.zeros_like(flat)
    period = feat * GROUP // LANES
    groups = c1 // GROUP
    at = iota((groups, LANES), 1)
    for j in range(period):
        chan, off = divmod(j * LANES, feat)
        lo = first_lo[pl.ds(chan, groups, stride=GROUP), :]
        hi = first_hi[pl.ds(chan, groups, stride=GROUP), :]
        value = pltpu.roll(hi, (-off) % LANES, 1)
        if off < LANES:
            lo_part = pltpu.roll(lo, (-off) % LANES, 1) if off else lo
            value = jnp.where(at < LANES - off, lo_part, value)
        if off + LANES > feat:
            after = first_lo[pl.ds(chan + 1, groups, stride=GROUP), :]
            value = jnp.where(at < feat - off, value, pltpu.roll(after, (feat - off) % LANES, 1))
        flat[pl.ds(j, groups, stride=period), :] = value
    base = c1 * feat // LANES
    half = LANES // 2
    second_s[...] = jnp.zeros_like(second_s)
    second_s[0:c2, 0:half] = acc_second[...]
    third_s[0:c2, :] = acc_third[...]
    third_s[c2 : c2 + 1, :] = d_head
    second_s[c2 : c2 + 1, :] = third_s[0:1, :]
    one = iota((1, LANES), 1) < half
    flat[base : base + 1, :] = jnp.concatenate(tap_rows[0:2], axis=1)
    flat[base + 1 : base + 2, :] = jnp.where(
        one,
        jnp.concatenate([tap_rows[2], tap_rows[2]], axis=1),
        pltpu.roll(second_s[0:1, :], half, 1),
    )
    odd = second_s[pl.ds(1, c2 // 2, stride=2), :]
    even = second_s[pl.ds(2, c2 // 2, stride=2), :]
    low = iota((c2 // 2, LANES), 1) < half
    flat[base + 2 : base + 2 + c2 // 2, :] = jnp.where(low, odd, pltpu.roll(even, half, 1))
    start = base + 2 + c2 // 2
    low = iota((c2, LANES), 1) < half
    flat[start : start + c2, :] = jnp.where(
        low, pltpu.roll(third_s[0:c2, :], half, 1), pltpu.roll(third_s[1 : c2 + 1, :], half, 1)
    )
    flat[start + c2 : start + c2 + 1, :] = jnp.where(one, pltpu.roll(d_head, half, 1), 0.0)

    def share_of(index):
        return pl.ds(pl.multiple_of(index * share, share), share)

    copies = []
    for by in range(1, n_tile):
        peer = tile_peer(by)
        copies.append(
            pltpu.make_async_remote_copy(
                src_ref=flat.at[share_of(peer)],
                dst_ref=parts.at[by - 1],
                send_sem=part_send.at[by - 1],
                recv_sem=part_recv.at[by - 1],
                device_id={"tile": peer},
                device_id_type=MESH,
            )
        )
        copies[-1].start()
    piece = flat[share_of(me), :]
    for n, copy in enumerate(copies):
        copy.wait_recv()
        piece = piece + parts[n]
    zparts[my_state] = piece
    zcopies = []
    for by in range(1, n_state):
        zcopies.append(
            pltpu.make_async_remote_copy(
                src_ref=zparts.at[my_state],
                dst_ref=zparts.at[my_state],
                send_sem=z_send.at[by - 1],
                recv_sem=z_recv.at[by - 1],
                device_id={"state": state_peer(by)},
                device_id_type=MESH,
            )
        )
        zcopies[-1].start()
    for copy in zcopies:
        copy.wait_recv()
    piece = zparts[0]
    for s in range(1, n_state):
        piece = piece + zparts[s]
    whole[share_of(me), :] = piece
    acopies = []
    for by in range(1, n_tile):
        acopies.append(
            pltpu.make_async_remote_copy(
                src_ref=whole.at[share_of(me)],
                dst_ref=whole.at[share_of(me)],
                send_sem=all_send.at[by - 1],
                recv_sem=all_recv.at[by - 1],
                device_id={"tile": tile_peer(by)},
                device_id_type=MESH,
            )
        )
        acopies[-1].start()
    for copy in copies:
        copy.wait_send()
    for copy in zcopies:
        copy.wait_send()
    for copy in acopies:
        copy.wait_recv()
    for copy in acopies:
        copy.wait_send()
    grads_out[...] = whole[...]


def on_device(
    n_tile, n_state,
    bands, block_slot, tile_counties, county_place, label, w_first, taps, w_second, w_third, w_head,
):
    feat, pixels = bands.shape[1:]
    c1, c2 = w_first.shape[0], w_second.shape[0]
    blocks = block_slot.shape[1]
    grads = c1 * feat + 3 * c1 + c2 * c1 + c2 * c2 + c2
    rows = pl.cdiv(grads, LANES)
    share = pl.cdiv(rows, n_tile * GROUP) * GROUP
    vmem = pl.BlockSpec(memory_space=pltpu.VMEM)
    dma = pltpu.SemaphoreType.DMA
    near = 2 * (REACH - 1)
    mean, out = pl.pallas_call(
        functools.partial(kernel, n_tile, n_state, share),
        out_shape=(
            jax.ShapeDtypeStruct(label.shape, F32),
            jax.ShapeDtypeStruct((n_tile * share, LANES), F32),
        ),
        in_specs=[pl.BlockSpec(memory_space=pl.ANY)] + [vmem] * 9,
        out_specs=(vmem, vmem),
        scratch_shapes=[
            pltpu.VMEM((feat, pixels), BF16),
            pltpu.VMEM((c1, pixels), BF16),
            pltpu.VMEM((c2, pixels), BF16),
            pltpu.VMEM((c1, pixels), F32),
            pltpu.VMEM((c2, pixels), F32),
            pltpu.VMEM((c2, pixels), F32),
            pltpu.VMEM((blocks, LANES), F32),
            pltpu.VMEM((blocks, LANES), F32),
            pltpu.VMEM((c2, c1), BF16),
            pltpu.VMEM((c1, c2), BF16),
            pltpu.VMEM((c2, c2), BF16),
            pltpu.VMEM((c2, c2), BF16),
            pltpu.VMEM((c2, LANES), F32),
            pltpu.VMEM((3 * c1, feat), F32),
            pltpu.VMEM((c2, c1), F32),
            pltpu.VMEM((c2, c2), F32),
            pltpu.VMEM((2 * GROUP, c2), F32),
            pltpu.VMEM((c1, LANES), F32),
            pltpu.VMEM((c1, LANES), F32),
            pltpu.VMEM((c2 + GROUP, LANES), F32),
            pltpu.VMEM((c2 + GROUP, LANES), F32),
            pltpu.VMEM((n_tile * share, LANES), F32),
            pltpu.VMEM((GROUP, LANES), F32),
            pltpu.VMEM((near, GROUP, LANES), F32),
            pltpu.VMEM((n_tile - 1, share, LANES), F32),
            pltpu.VMEM((n_state, share, LANES), F32),
            pltpu.VMEM((n_tile * share, LANES), F32),
            dma((DMA_STEPS,)),
            dma((near,)),
            dma((near,)),
            dma((n_tile - 1,)),
            dma((n_tile - 1,)),
            dma((n_state - 1,)),
            dma((n_state - 1,)),
            dma((n_tile - 1,)),
            dma((n_tile - 1,)),
        ],
        compiler_params=pltpu.CompilerParams(
            collective_id=0, has_side_effects=True, vmem_limit_bytes=56 * 2**20
        ),
    )(
        bands, block_slot, tile_counties, county_place, label,
        w_first, taps, w_second.T, w_third, w_head.reshape(1, -1),
    )
    return mean, out.reshape(-1)[:grads]


def solution(mesh):
    in_specs = (
        P("state", None, "tile"),
        P("state", "tile"),
        P("state", "tile"),
        P("state", None),
        P("state", "tile"),
        P(),
        P(),
        P(),
        P(),
        P(),
    )
    return jax.shard_map(
        functools.partial(on_device, mesh.shape["tile"], mesh.shape["state"]),
        mesh=mesh,
        in_specs=in_specs,
        out_specs=(P("state", "tile"), P()),
        check_vma=False,
    )
```

```python
import functools

import jax
import jax.numpy as jnp
from jax import lax
from jax.experimental import pallas as pl
from jax.experimental.pallas import tpu as pltpu
from jax.sharding import PartitionSpec as P

REACH = 4
LANES = 128
GROUP = 8
STEP_ROWS = 32
MESH = pl.DeviceIdType.MESH
F32 = jnp.float32
BF16 = jnp.bfloat16


def mm(left, right):
    return jnp.dot(left, right, preferred_element_type=F32)


def mm_last(left, right):
    return lax.dot_general(left, right, (((1,), (1,)), ((), ())), preferred_element_type=F32)


def iota(shape, dim):
    return lax.broadcasted_iota(jnp.int32, shape, dim)


def to_column(row, size):
    eye = iota((size, size), 0) == iota((size, size), 1)
    return jnp.sum(jnp.where(eye, row, 0.0), axis=1, keepdims=True)


def to_row(column, size):
    eye = iota((size, size), 0) == iota((size, size), 1)
    return jnp.sum(jnp.where(eye, column, 0.0), axis=0, keepdims=True)


def gate_parts(half):
    twice = jnp.tanh(half) + 1.0
    act = half * twice
    return act, twice + act * (2.0 - twice)


def kernel(
    n_tile, n_state, share_lo, share_hi,
    bands, slot_row, counties, table, label, w_first, taps, w_second, w_third, w_head,
    mean_out, grads_out,
    x_s, a1_s, a2_s, d1_s, d2_s, u3_s, u2_s, u1_s, slot_s, g_s, w2_s, w2t_s, w3_s, w3t_s, wh_s,
    acc_first, acc_second, acc_third, acc_head, first_lo, first_hi, second_s, third_s, tail,
    msg, msgs, flat_lo, flat_hi, parts_lo, parts_hi, zparts_lo, zparts_hi, whole_lo, whole_hi,
    x_sem, msg_send, msg_recv, *sum_sems,
):
    me = lax.axis_index("tile")
    my_state = lax.axis_index("state")
    c1, feat = w_first.shape
    c2 = w_second.shape[1]
    blocks = slot_row.shape[1]
    pixels = bands.shape[2]
    row_len = pixels // blocks
    cty_dev = label.shape[1]
    places = table.shape[1]
    slot_count = counties.shape[1]
    step_px = STEP_ROWS * row_len
    steps = pixels // step_px

    def band_copy(k):
        cols = pl.ds(pl.multiple_of(k * step_px, step_px), step_px)
        return pltpu.make_async_copy(bands.at[0, :, cols], x_s.at[:, cols], x_sem.at[k])

    for k in range(steps):
        band_copy(k).start()

    def tile_peer(by):
        return lax.rem(me + by + n_tile, n_tile)

    def state_peer(by):
        return lax.rem(my_state + by + n_state, n_state)

    barrier = pltpu.get_barrier_semaphore()
    for by in range(1, n_tile):
        pl.semaphore_signal(barrier, inc=1, device_id={"tile": tile_peer(by)}, device_id_type=MESH)
    for by in range(1, n_state):
        pl.semaphore_signal(
            barrier, inc=1, device_id={"state": state_peer(by)}, device_id_type=MESH
        )

    slots = slot_row[...].astype(F32)
    slot_s[...] = jnp.broadcast_to(to_column(slots, blocks), (blocks, LANES))
    half_second = w_second[...].astype(F32) * 0.5
    half_third = w_third[...].astype(F32) * 0.5
    w2t_s[...] = half_second.astype(BF16)
    w3_s[...] = half_third.astype(BF16)
    w2_s[...] = half_second.T.astype(BF16)
    w3t_s[...] = half_third.T.astype(BF16)
    head_row = w_head[...].astype(F32)
    wh_s[...] = jnp.broadcast_to(to_column(head_row, c2) * 0.5, (c2, LANES))
    tap_cols = [to_column(taps[k : k + 1, :], c1) for k in range(3)]
    lane = iota((c1, LANES), 1)
    tap_prev = jnp.where(lane == 0, 0.0, tap_cols[0] * 0.5)
    tap_here = jnp.broadcast_to(tap_cols[1] * 0.5, (c1, LANES))
    tap_next = jnp.where(lane == LANES - 1, 0.0, tap_cols[2] * 0.5)
    acc_first[...] = jnp.zeros_like(acc_first)
    acc_second[...] = jnp.zeros_like(acc_second)
    acc_third[...] = jnp.zeros_like(acc_third)
    acc_head[...] = jnp.zeros_like(acc_head)
    slot_ids = iota((2 * GROUP, LANES), 0).astype(F32)

    def row_cols(j):
        return slice(j * row_len, (j + 1) * row_len)

    def all_rows(tile):
        return jnp.concatenate([tile] * STEP_ROWS, axis=1)

    def forward(step, carry):
        band_copy(step).wait()
        cols = pl.ds(pl.multiple_of(step * step_px, step_px), step_px)
        h1 = mm(w_first[...], x_s[:, cols])
        s1 = []
        for j in range(STEP_ROWS):
            h = h1[:, row_cols(j)]
            s1.append(
                tap_prev * pltpu.roll(h, 1, 1)
                + tap_here * h
                + tap_next * pltpu.roll(h, LANES - 1, 1)
            )
        a1, d1 = gate_parts(jnp.concatenate(s1, axis=1))
        d1_s[:, cols] = d1
        a1 = a1.astype(BF16)
        a1_s[:, cols] = a1
        a2, d2 = gate_parts(mm(w2_s[...], a1))
        d2_s[:, cols] = d2
        a2 = a2.astype(BF16)
        a2_s[:, cols] = a2
        a3, d3 = gate_parts(mm(w3_s[...], a2))
        u3_s[:, cols] = (all_rows(wh_s[...]) * d3).astype(BF16)
        a3 = (a3 + a2.astype(F32)).astype(BF16)
        member = jnp.concatenate(
            [
                (slot_s[pl.ds(step * STEP_ROWS + j, 1), :] == slot_ids).astype(F32)
                for j in range(STEP_ROWS)
            ],
            axis=1,
        ).astype(BF16)
        acc_head[...] += mm_last(member, a3)
        return carry

    lax.fori_loop(0, steps, forward, 0)

    head_sums = acc_head[0:GROUP, :]
    slot_sums = jnp.sum(head_sums * head_row, axis=1, keepdims=True)
    in_slot = (slots == slot_ids[0:GROUP, :]).astype(F32)
    slot_counts = jnp.sum(in_slot, axis=1, keepdims=True) * float(row_len)
    county = to_column(counties[...].astype(F32), slot_count)
    hits = county == iota((slot_count, places), 1).astype(F32)
    place = jnp.sum(jnp.where(hits, table[...].astype(F32), 0.0), axis=1, keepdims=True)
    place = place - (me * cty_dev).astype(F32)
    place = jnp.where(place < 0.0, place + float(places), place)
    pick = (place == iota((slot_count, LANES), 1).astype(F32)).astype(F32)
    msg[...] = jnp.zeros_like(msg)
    msg[0:1, :] = jnp.sum(pick * slot_sums, axis=0, keepdims=True)
    msg[1:2, :] = jnp.sum(pick * slot_counts, axis=0, keepdims=True)
    msg[2:3, 0:cty_dev] = label[...].astype(F32)

    pl.semaphore_wait(barrier, n_tile - 1 + n_state - 1)
    offsets = [by for by in range(1 - REACH, REACH) if by]
    copies = []
    for n, by in enumerate(offsets):
        copies.append(
            pltpu.make_async_remote_copy(
                src_ref=msg,
                dst_ref=msgs.at[n],
                send_sem=msg_send.at[n],
                recv_sem=msg_recv.at[n],
                device_id={"tile": tile_peer(by)},
                device_id_type=MESH,
            )
        )
        copies[-1].start()

    def backward(step, carry):
        cols = pl.ds(pl.multiple_of(step * step_px, step_px), step_px)
        u2 = ((mm(w3t_s[...], u3_s[:, cols]) + all_rows(wh_s[...])) * d2_s[:, cols]).astype(BF16)
        u2_s[:, cols] = u2
        u1 = mm(w2t_s[...], u2) * d1_s[:, cols]
        left, right = [], []
        for j in range(STEP_ROWS):
            d = u1[:, row_cols(j)]
            left.append(jnp.where(lane == LANES - 1, 0.0, pltpu.roll(d, LANES - 1, 1)))
            right.append(jnp.where(lane == 0, 0.0, pltpu.roll(d, 1, 1)))
        u1_s[0:c1, cols] = jnp.concatenate(left, axis=1).astype(BF16)
        u1_s[c1 : 2 * c1, cols] = u1.astype(BF16)
        u1_s[2 * c1 : 3 * c1, cols] = jnp.concatenate(right, axis=1).astype(BF16)
        return carry

    lax.fori_loop(0, steps, backward, 0)

    total = msg[...]
    for n, by in enumerate(offsets):
        copies[n].wait_recv()
        total = total + pltpu.roll(msgs[n], (-by * cty_dev) % LANES, 1)
    for copy in copies:
        copy.wait_send()
    sums, counts, target = total[0:1, :], total[1:2, :], total[2:3, :] * 0.01
    denom = jnp.maximum(counts, 1.0)
    mean = sums / denom
    mean_out[...] = mean[:, 0:cty_dev]
    adjoint = jnp.where(
        counts > 0.5, 2.0 * (mean - target) / (float(n_tile * n_state) * denom), 0.0
    )
    slot_g = jnp.sum(jnp.where(pick > 0.5, adjoint, 0.0), axis=1, keepdims=True)
    slot_g = slot_g.astype(BF16).astype(F32)
    all_slots = slot_s[...]
    g_rows = jnp.zeros((blocks, LANES), F32)
    for s in range(slot_count):
        g_rows = jnp.where(all_slots == float(s), slot_g[s : s + 1, 0:1], g_rows)
    g_s[...] = g_rows

    def g_tile(step, chans):
        rows = []
        for j in range(STEP_ROWS):
            row = jnp.broadcast_to(g_s[pl.ds(step * STEP_ROWS + j, 1), :], (2 * GROUP, LANES))
            rows.append(jnp.concatenate([row.astype(BF16)] * (chans // (2 * GROUP)), axis=0))
        return jnp.concatenate(rows, axis=1)

    def deep_grads(step, carry):
        cols = pl.ds(pl.multiple_of(step * step_px, step_px), step_px)
        g = g_tile(step, c2)
        acc_third[...] += mm_last(u3_s[:, cols] * g, a2_s[:, cols])
        acc_second[...] += mm_last(u2_s[:, cols] * g, a1_s[:, cols])
        return carry

    def first_grads(step, carry):
        cols = pl.ds(pl.multiple_of(step * step_px, step_px), step_px)
        acc_first[...] += mm_last(u1_s[:, cols] * g_tile(step, 3 * c1), x_s[:, cols])
        return carry

    def summing(share, flat, parts, zparts, whole, part_send, part_recv, z_send, z_recv, all_send, all_recv):
        def share_of(index):
            return pl.ds(pl.multiple_of(index * share, share), share)

        scatter, across, gather = [], [], []
        for by in range(1, n_tile):
            peer = tile_peer(by)
            where = {"tile": peer}
            scatter.append(
                pltpu.make_async_remote_copy(
                    src_ref=flat.at[share_of(peer)],
                    dst_ref=parts.at[by - 1],
                    send_sem=part_send.at[by - 1],
                    recv_sem=part_recv.at[by - 1],
                    device_id=where,
                    device_id_type=MESH,
                )
            )
            gather.append(
                pltpu.make_async_remote_copy(
                    src_ref=whole.at[share_of(me)],
                    dst_ref=whole.at[share_of(me)],
                    send_sem=all_send.at[by - 1],
                    recv_sem=all_recv.at[by - 1],
                    device_id=where,
                    device_id_type=MESH,
                )
            )
        for by in range(1, n_state):
            across.append(
                pltpu.make_async_remote_copy(
                    src_ref=zparts.at[my_state],
                    dst_ref=zparts.at[my_state],
                    send_sem=z_send.at[by - 1],
                    recv_sem=z_recv.at[by - 1],
                    device_id={"state": state_peer(by)},
                    device_id_type=MESH,
                )
            )

        def first():
            for copy in scatter:
                copy.start()

        def second():
            piece = flat[share_of(me), :]
            for n, copy in enumerate(scatter):
                copy.wait_recv()
                piece = piece + parts[n]
            zparts[my_state] = piece
            for copy in across:
                copy.start()

        def third():
            for copy in across:
                copy.wait_recv()
            piece = zparts[0]
            for s in range(1, n_state):
                piece = piece + zparts[s]
            whole[share_of(me), :] = piece
            for copy in gather:
                copy.start()

        def last():
            for copy in gather:
                copy.wait_recv()
            for copy in scatter + across + gather:
                copy.wait_send()

        return first, second, third, last

    lo = summing(share_lo, flat_lo, parts_lo, zparts_lo, whole_lo, *sum_sems[0:6])
    hi = summing(share_hi, flat_hi, parts_hi, zparts_hi, whole_hi, *sum_sems[6:12])

    lax.fori_loop(0, steps, deep_grads, 0)

    base = c1 * feat // LANES
    half = LANES // 2
    d_head = jnp.sum(head_sums * slot_g, axis=0, keepdims=True)
    second_s[...] = jnp.zeros_like(second_s)
    second_s[0:c2, 0:half] = acc_second[...]
    third_s[0:c2, :] = acc_third[...]
    third_s[c2 : c2 + 1, :] = d_head
    second_s[c2 : c2 + 1, :] = third_s[0:1, :]
    one = iota((1, LANES), 1) < half
    tail[...] = jnp.zeros_like(tail)
    tail[1:2, :] = pltpu.roll(second_s[0:1, :], half, 1)
    odd = second_s[pl.ds(1, c2 // 2, stride=2), :]
    even = second_s[pl.ds(2, c2 // 2, stride=2), :]
    low = iota((c2 // 2, LANES), 1) < half
    tail[2 : 2 + c2 // 2, :] = jnp.where(low, odd, pltpu.roll(even, half, 1))
    start = 2 + c2 // 2
    low = iota((c2, LANES), 1) < half
    tail[start : start + c2, :] = jnp.where(
        low, pltpu.roll(third_s[0:c2, :], half, 1), pltpu.roll(third_s[1 : c2 + 1, :], half, 1)
    )
    tail[start + c2 : start + c2 + 1, :] = jnp.where(one, pltpu.roll(d_head, half, 1), 0.0)
    flat_hi[...] = tail[GROUP:, :]
    hi[0]()
    lax.fori_loop(0, steps // 2, first_grads, 0)
    hi[1]()
    lax.fori_loop(steps // 2, steps, first_grads, 0)
    hi[2]()

    g_first = [acc_first[k * c1 : (k + 1) * c1, :] for k in range(3)]
    weights = w_first[...].astype(F32)
    d_first = tap_cols[0] * g_first[0] + tap_cols[1] * g_first[1] + tap_cols[2] * g_first[2]
    tap_rows = [
        to_row(jnp.sum(weights * g, axis=1, keepdims=True), c1) for g in g_first
    ]
    first_lo[...] = d_first[:, 0:LANES]
    first_hi[:, 0 : feat - LANES] = d_first[:, LANES:feat]
    period = feat * GROUP // LANES
    groups = c1 // GROUP
    at = iota((groups, LANES), 1)
    flat_lo[...] = jnp.zeros_like(flat_lo)
    for j in range(period):
        chan, off = divmod(j * LANES, feat)
        lows = first_lo[pl.ds(chan, groups, stride=GROUP), :]
        highs = first_hi[pl.ds(chan, groups, stride=GROUP), :]
        value = pltpu.roll(highs, (-off) % LANES, 1)
        if off < LANES:
            shifted = pltpu.roll(lows, (-off) % LANES, 1) if off else lows
            value = jnp.where(at < LANES - off, shifted, value)
        if off + LANES > feat:
            after = first_lo[pl.ds(chan + 1, groups, stride=GROUP), :]
            value = jnp.where(at < feat - off, value, pltpu.roll(after, (feat - off) % LANES, 1))
        flat_lo[pl.ds(j, groups, stride=period), :] = value
    tail[0:1, :] = jnp.concatenate(tap_rows[0:2], axis=1)
    tail[1:2, :] = jnp.where(one, jnp.concatenate([tap_rows[2], tap_rows[2]], axis=1), tail[1:2, :])
    flat_lo[base : base + GROUP, :] = tail[0:GROUP, :]
    for phase in lo:
        phase()
    hi[3]()
    split = base + GROUP
    grads_out[0:split, :] = whole_lo[0:split, :]
    grads_out[split:, :] = whole_hi[...]


def on_device(
    n_tile, n_state,
    bands, block_slot, tile_counties, county_place, label, w_first, taps, w_second, w_third, w_head,
):
    feat, pixels = bands.shape[1:]
    c1, c2 = w_first.shape[0], w_second.shape[0]
    blocks = block_slot.shape[1]
    grads = c1 * feat + 3 * c1 + c2 * c1 + c2 * c2 + c2
    rows = pl.cdiv(grads, LANES)
    split = c1 * feat // LANES + GROUP
    share_lo = pl.cdiv(split, n_tile * GROUP) * GROUP
    share_hi = pl.cdiv(rows - split, n_tile * GROUP) * GROUP
    rows_lo, rows_hi = n_tile * share_lo, n_tile * share_hi
    steps = blocks // STEP_ROWS
    vmem = pl.BlockSpec(memory_space=pltpu.VMEM)
    dma = pltpu.SemaphoreType.DMA
    near = 2 * (REACH - 1)
    mean, out = pl.pallas_call(
        functools.partial(kernel, n_tile, n_state, share_lo, share_hi),
        out_shape=(
            jax.ShapeDtypeStruct(label.shape, F32),
            jax.ShapeDtypeStruct((split + rows_hi, LANES), F32),
        ),
        in_specs=[pl.BlockSpec(memory_space=pl.ANY)] + [vmem] * 9,
        out_specs=(vmem, vmem),
        scratch_shapes=[
            pltpu.VMEM((feat, pixels), BF16),
            pltpu.VMEM((c1, pixels), BF16),
            pltpu.VMEM((c2, pixels), BF16),
            pltpu.VMEM((c1, pixels), F32),
            pltpu.VMEM((c2, pixels), F32),
            pltpu.VMEM((c2, pixels), BF16),
            pltpu.VMEM((c2, pixels), BF16),
            pltpu.VMEM((3 * c1, pixels), BF16),
            pltpu.VMEM((blocks, LANES), F32),
            pltpu.VMEM((blocks, LANES), F32),
            pltpu.VMEM((c2, c1), BF16),
            pltpu.VMEM((c1, c2), BF16),
            pltpu.VMEM((c2, c2), BF16),
            pltpu.VMEM((c2, c2), BF16),
            pltpu.VMEM((c2, LANES), F32),
            pltpu.VMEM((3 * c1, feat), F32),
            pltpu.VMEM((c2, c1), F32),
            pltpu.VMEM((c2, c2), F32),
            pltpu.VMEM((2 * GROUP, c2), F32),
            pltpu.VMEM((c1, LANES), F32),
            pltpu.VMEM((c1, LANES), F32),
            pltpu.VMEM((c2 + GROUP, LANES), F32),
            pltpu.VMEM((c2 + GROUP, LANES), F32),
            pltpu.VMEM((GROUP + rows_hi, LANES), F32),
            pltpu.VMEM((GROUP, LANES), F32),
            pltpu.VMEM((near, GROUP, LANES), F32),
            pltpu.VMEM((rows_lo, LANES), F32),
            pltpu.VMEM((rows_hi, LANES), F32),
            pltpu.VMEM((n_tile - 1, share_lo, LANES), F32),
            pltpu.VMEM((n_tile - 1, share_hi, LANES), F32),
            pltpu.VMEM((n_state, share_lo, LANES), F32),
            pltpu.VMEM((n_state, share_hi, LANES), F32),
            pltpu.VMEM((rows_lo, LANES), F32),
            pltpu.VMEM((rows_hi, LANES), F32),
            dma((steps,)),
            dma((near,)),
            dma((near,)),
        ]
        + [
            dma((peers,))
            for peers in (n_tile - 1, n_tile - 1, n_state - 1, n_state - 1, n_tile - 1, n_tile - 1) * 2
        ],
        compiler_params=pltpu.CompilerParams(
            collective_id=0, has_side_effects=True, vmem_limit_bytes=56 * 2**20
        ),
    )(
        bands, block_slot, tile_counties, county_place, label,
        w_first, taps, w_second.T, w_third, w_head.reshape(1, -1),
    )
    return mean, out.reshape(-1)[:grads]


def solution(mesh):
    in_specs = (
        P("state", None, "tile"),
        P("state", "tile"),
        P("state", "tile"),
        P("state", None),
        P("state", "tile"),
        P(),
        P(),
        P(),
        P(),
        P(),
    )
    return jax.shard_map(
        functools.partial(on_device, mesh.shape["tile"], mesh.shape["state"]),
        mesh=mesh,
        in_specs=in_specs,
        out_specs=(P("state", "tile"), P()),
        check_vma=False,
    )
```

```python
import functools

import jax
import jax.numpy as jnp
from jax import lax
from jax.experimental import pallas as pl
from jax.experimental.pallas import tpu as pltpu
from jax.sharding import PartitionSpec as P

REACH = 4
LANES = 128
GROUP = 8
STEP_ROWS = 32
TICK_ROWS = 2
SUM_ROWS = 8
MESH = pl.DeviceIdType.MESH
F32 = jnp.float32
BF16 = jnp.bfloat16


def mm(left, right):
    return jnp.dot(left, right, preferred_element_type=F32)


def mm_last(left, right):
    return lax.dot_general(left, right, (((1,), (1,)), ((), ())), preferred_element_type=F32)


def iota(shape, dim):
    return lax.broadcasted_iota(jnp.int32, shape, dim)


def to_column(row, size):
    eye = iota((size, size), 0) == iota((size, size), 1)
    return jnp.sum(jnp.where(eye, row, 0.0), axis=1, keepdims=True)


def to_row(column, size):
    eye = iota((size, size), 0) == iota((size, size), 1)
    return jnp.sum(jnp.where(eye, column, 0.0), axis=0, keepdims=True)


def gate_parts(half):
    twice = jnp.tanh(half) + 1.0
    act = half * twice
    return act, twice + act * (2.0 - twice)


def kernel(
    n_tile, n_state, share_lo, share_hi,
    bands, slot_row, counties, table, label, w_first, taps, w_second, w_third, w_head,
    mean_out, grads_out,
    x_s, a1_s, a2_s, d1_s, d2_s, u3_s, u2_s, u1_s, slot_s, g_s, w2_s, w2t_s, w3_s, w3t_s, wh_s,
    acc_first, acc_second, acc_third, acc_head, first_lo, first_hi, second_s, third_s, tail,
    msg, msgs, flat_lo, flat_hi, parts_lo, parts_hi, zparts_lo, zparts_hi, whole_lo, whole_hi,
    x_sem, msg_send, msg_recv, *sum_sems,
):
    me = lax.axis_index("tile")
    my_state = lax.axis_index("state")
    c1, feat = w_first.shape
    c2 = w_second.shape[1]
    blocks = slot_row.shape[1]
    pixels = bands.shape[2]
    row_len = pixels // blocks
    cty_dev = label.shape[1]
    places = table.shape[1]
    slot_count = counties.shape[1]
    step_px = STEP_ROWS * row_len
    steps = pixels // step_px

    def band_copy(k):
        cols = pl.ds(pl.multiple_of(k * step_px, step_px), step_px)
        return pltpu.make_async_copy(bands.at[0, :, cols], x_s.at[:, cols], x_sem.at[k])

    for k in range(steps):
        band_copy(k).start()

    def tile_peer(by):
        return lax.rem(me + by + n_tile, n_tile)

    def state_peer(by):
        return lax.rem(my_state + by + n_state, n_state)

    barrier = pltpu.get_barrier_semaphore()
    for by in range(1, n_tile):
        pl.semaphore_signal(barrier, inc=1, device_id={"tile": tile_peer(by)}, device_id_type=MESH)
    for by in range(1, n_state):
        pl.semaphore_signal(
            barrier, inc=1, device_id={"state": state_peer(by)}, device_id_type=MESH
        )

    slots = slot_row[...].astype(F32)
    slot_s[...] = jnp.broadcast_to(to_column(slots, blocks), (blocks, LANES))
    half_second = w_second[...].astype(F32) * 0.5
    half_third = w_third[...].astype(F32) * 0.5
    w2t_s[...] = half_second.astype(BF16)
    w3_s[...] = half_third.astype(BF16)
    w2_s[...] = half_second.T.astype(BF16)
    w3t_s[...] = half_third.T.astype(BF16)
    head_row = w_head[...].astype(F32)
    wh_s[...] = jnp.broadcast_to(to_column(head_row, c2) * 0.5, (c2, LANES))
    tap_cols = [to_column(taps[k : k + 1, :], c1) for k in range(3)]
    lane = iota((c1, LANES), 1)
    tap_prev = jnp.where(lane == 0, 0.0, tap_cols[0] * 0.5)
    tap_here = jnp.broadcast_to(tap_cols[1] * 0.5, (c1, LANES))
    tap_next = jnp.where(lane == LANES - 1, 0.0, tap_cols[2] * 0.5)
    acc_first[...] = jnp.zeros_like(acc_first)
    acc_second[...] = jnp.zeros_like(acc_second)
    acc_third[...] = jnp.zeros_like(acc_third)
    acc_head[...] = jnp.zeros_like(acc_head)
    slot_ids = iota((2 * GROUP, LANES), 0).astype(F32)

    def row_cols(j):
        return slice(j * row_len, (j + 1) * row_len)

    ticks = STEP_ROWS // TICK_ROWS
    tick_px = TICK_ROWS * row_len

    def columns(step, tick, j=None):
        first = step * step_px + tick * tick_px + (0 if j is None else j * row_len)
        size = tick_px if j is None else row_len
        return pl.ds(pl.multiple_of(first, row_len), size)

    def skewed(stages):
        held = [None] * len(stages)
        for now in range(ticks + len(stages) - 1):
            for n in reversed(range(len(stages))):
                tick = now - n
                if 0 <= tick < ticks:
                    held[n] = stages[n](tick, held[n - 1] if n else None)

    def halves():
        return [slice(r, r + c1) for r in range(0, c2, c1)]

    def forward(step, carry):
        band_copy(step).wait()
        head = [acc_head[...]]

        def stage_one(tick, _):
            return mm(w_first[...], x_s[:, columns(step, tick)])

        def stage_two(tick, h1):
            tiles = []
            for j in range(TICK_ROWS):
                h = h1[:, row_cols(j)]
                s1 = (
                    tap_prev * pltpu.roll(h, 1, 1)
                    + tap_here * h
                    + tap_next * pltpu.roll(h, LANES - 1, 1)
                )
                act, d1_s[:, columns(step, tick, j)] = gate_parts(s1)
                act = act.astype(BF16)
                a1_s[:, columns(step, tick, j)] = act
                tiles.append(act)
            return mm(w2_s[...], jnp.concatenate(tiles, axis=1))

        def stage_three(tick, h2):
            tiles = []
            for j in range(TICK_ROWS):
                parts = []
                for part in halves():
                    act, d2_s[part, columns(step, tick, j)] = gate_parts(h2[part, row_cols(j)])
                    act = act.astype(BF16)
                    a2_s[part, columns(step, tick, j)] = act
                    parts.append(act)
                tiles.append(jnp.concatenate(parts, axis=0))
            return mm(w3_s[...], jnp.concatenate(tiles, axis=1))

        def stage_four(tick, h3):
            tiles, members = [], []
            for j in range(TICK_ROWS):
                parts = []
                for part in halves():
                    act, d3 = gate_parts(h3[part, row_cols(j)])
                    u3_s[part, columns(step, tick, j)] = (wh_s[part, :] * d3).astype(BF16)
                    a2 = a2_s[part, columns(step, tick, j)].astype(F32)
                    parts.append((act + a2).astype(BF16))
                tiles.append(jnp.concatenate(parts, axis=0))
                row = slot_s[pl.ds(step * STEP_ROWS + tick * TICK_ROWS + j, 1), :]
                members.append((row == slot_ids).astype(F32).astype(BF16))
            head[0] = head[0] + mm_last(
                jnp.concatenate(members, axis=1), jnp.concatenate(tiles, axis=1)
            )

        skewed([stage_one, stage_two, stage_three, stage_four])
        acc_head[...] = head[0]
        return carry

    lax.fori_loop(0, steps, forward, 0)

    head_sums = acc_head[0:GROUP, :]
    slot_sums = jnp.sum(head_sums * head_row, axis=1, keepdims=True)
    in_slot = (slots == slot_ids[0:GROUP, :]).astype(F32)
    slot_counts = jnp.sum(in_slot, axis=1, keepdims=True) * float(row_len)
    county = to_column(counties[...].astype(F32), slot_count)
    hits = county == iota((slot_count, places), 1).astype(F32)
    place = jnp.sum(jnp.where(hits, table[...].astype(F32), 0.0), axis=1, keepdims=True)
    place = place - (me * cty_dev).astype(F32)
    place = jnp.where(place < 0.0, place + float(places), place)
    pick = (place == iota((slot_count, LANES), 1).astype(F32)).astype(F32)
    msg[...] = jnp.zeros_like(msg)
    msg[0:1, :] = jnp.sum(pick * slot_sums, axis=0, keepdims=True)
    msg[1:2, :] = jnp.sum(pick * slot_counts, axis=0, keepdims=True)
    msg[2:3, 0:cty_dev] = label[...].astype(F32)

    pl.semaphore_wait(barrier, n_tile - 1 + n_state - 1)
    offsets = [by for by in range(1 - REACH, REACH) if by]
    copies = []
    for n, by in enumerate(offsets):
        copies.append(
            pltpu.make_async_remote_copy(
                src_ref=msg,
                dst_ref=msgs.at[n],
                send_sem=msg_send.at[n],
                recv_sem=msg_recv.at[n],
                device_id={"tile": tile_peer(by)},
                device_id_type=MESH,
            )
        )
        copies[-1].start()

    def backward(step, carry):
        def stage_one(tick, _):
            return mm(w3t_s[...], u3_s[:, columns(step, tick)])

        def stage_two(tick, d_a2):
            tiles = []
            for j in range(TICK_ROWS):
                parts = []
                for part in halves():
                    d_h2 = (d_a2[part, row_cols(j)] + wh_s[part, :]) * d2_s[part, columns(step, tick, j)]
                    d_h2 = d_h2.astype(BF16)
                    u2_s[part, columns(step, tick, j)] = d_h2
                    parts.append(d_h2)
                tiles.append(jnp.concatenate(parts, axis=0))
            return mm(w2t_s[...], jnp.concatenate(tiles, axis=1))

        def stage_three(tick, d_a1):
            for j in range(TICK_ROWS):
                cols = columns(step, tick, j)
                d = d_a1[:, row_cols(j)] * d1_s[:, cols]
                u1_s[0:c1, cols] = jnp.where(
                    lane == LANES - 1, 0.0, pltpu.roll(d, LANES - 1, 1)
                ).astype(BF16)
                u1_s[c1 : 2 * c1, cols] = d.astype(BF16)
                u1_s[2 * c1 : 3 * c1, cols] = jnp.where(lane == 0, 0.0, pltpu.roll(d, 1, 1)).astype(
                    BF16
                )

        skewed([stage_one, stage_two, stage_three])
        return carry

    lax.fori_loop(0, steps, backward, 0)

    total = msg[...]
    for n, by in enumerate(offsets):
        copies[n].wait_recv()
        total = total + pltpu.roll(msgs[n], (-by * cty_dev) % LANES, 1)
    for copy in copies:
        copy.wait_send()
    sums, counts, target = total[0:1, :], total[1:2, :], total[2:3, :] * 0.01
    denom = jnp.maximum(counts, 1.0)
    mean = sums / denom
    mean_out[...] = mean[:, 0:cty_dev]
    adjoint = jnp.where(
        counts > 0.5, 2.0 * (mean - target) / (float(n_tile * n_state) * denom), 0.0
    )
    slot_g = jnp.sum(jnp.where(pick > 0.5, adjoint, 0.0), axis=1, keepdims=True)
    slot_g = slot_g.astype(BF16).astype(F32)
    all_slots = slot_s[...]
    g_rows = jnp.zeros((blocks, LANES), F32)
    for s in range(slot_count):
        g_rows = jnp.where(all_slots == float(s), slot_g[s : s + 1, 0:1], g_rows)
    g_s[...] = g_rows

    def scaled(field, first):
        tiles = []
        for j in range(SUM_ROWS):
            row = jnp.broadcast_to(g_s[pl.ds(first + j, 1), :], (2 * GROUP, LANES)).astype(BF16)
            tile = jnp.concatenate([row] * (field.shape[0] // (2 * GROUP)), axis=0)
            cols = pl.ds(pl.multiple_of((first + j) * row_len, row_len), row_len)
            tiles.append(field[:, cols] * tile)
        return jnp.concatenate(tiles, axis=1)

    def chunks(step):
        for n in range(STEP_ROWS // SUM_ROWS):
            first = step * STEP_ROWS + n * SUM_ROWS
            px = SUM_ROWS * row_len
            yield first, pl.ds(pl.multiple_of(first * row_len, px), px)

    def deep_grads(step, carry):
        third, second = acc_third[...], acc_second[...]
        for first, cols in chunks(step):
            third = third + mm_last(scaled(u3_s, first), a2_s[:, cols])
            second = second + mm_last(scaled(u2_s, first), a1_s[:, cols])
        acc_third[...] = third
        acc_second[...] = second
        return carry

    def first_grads(step, carry):
        for first, cols in chunks(step):
            acc_first[...] += mm_last(scaled(u1_s, first), x_s[:, cols])
        return carry

    def summing(share, flat, parts, zparts, whole, part_send, part_recv, z_send, z_recv, all_send, all_recv):
        def share_of(index):
            return pl.ds(pl.multiple_of(index * share, share), share)

        scatter, across, gather = [], [], []
        for by in range(1, n_tile):
            peer = tile_peer(by)
            where = {"tile": peer}
            scatter.append(
                pltpu.make_async_remote_copy(
                    src_ref=flat.at[share_of(peer)],
                    dst_ref=parts.at[by - 1],
                    send_sem=part_send.at[by - 1],
                    recv_sem=part_recv.at[by - 1],
                    device_id=where,
                    device_id_type=MESH,
                )
            )
            gather.append(
                pltpu.make_async_remote_copy(
                    src_ref=whole.at[share_of(me)],
                    dst_ref=whole.at[share_of(me)],
                    send_sem=all_send.at[by - 1],
                    recv_sem=all_recv.at[by - 1],
                    device_id=where,
                    device_id_type=MESH,
                )
            )
        for by in range(1, n_state):
            across.append(
                pltpu.make_async_remote_copy(
                    src_ref=zparts.at[my_state],
                    dst_ref=zparts.at[my_state],
                    send_sem=z_send.at[by - 1],
                    recv_sem=z_recv.at[by - 1],
                    device_id={"state": state_peer(by)},
                    device_id_type=MESH,
                )
            )

        def first():
            for copy in scatter:
                copy.start()

        def second():
            piece = flat[share_of(me), :]
            for n, copy in enumerate(scatter):
                copy.wait_recv()
                piece = piece + parts[n]
            zparts[my_state] = piece
            for copy in across:
                copy.start()

        def third():
            for copy in across:
                copy.wait_recv()
            piece = zparts[0]
            for s in range(1, n_state):
                piece = piece + zparts[s]
            whole[share_of(me), :] = piece
            for copy in gather:
                copy.start()

        def last():
            for copy in gather:
                copy.wait_recv()
            for copy in scatter + across + gather:
                copy.wait_send()

        return first, second, third, last

    lo = summing(share_lo, flat_lo, parts_lo, zparts_lo, whole_lo, *sum_sems[0:6])
    hi = summing(share_hi, flat_hi, parts_hi, zparts_hi, whole_hi, *sum_sems[6:12])

    lax.fori_loop(0, steps, deep_grads, 0)

    base = c1 * feat // LANES
    half = LANES // 2
    d_head = jnp.sum(head_sums * slot_g, axis=0, keepdims=True)
    second_s[...] = jnp.zeros_like(second_s)
    second_s[0:c2, 0:half] = acc_second[...]
    third_s[0:c2, :] = acc_third[...]
    third_s[c2 : c2 + 1, :] = d_head
    second_s[c2 : c2 + 1, :] = third_s[0:1, :]
    one = iota((1, LANES), 1) < half
    tail[...] = jnp.zeros_like(tail)
    tail[1:2, :] = pltpu.roll(second_s[0:1, :], half, 1)
    odd = second_s[pl.ds(1, c2 // 2, stride=2), :]
    even = second_s[pl.ds(2, c2 // 2, stride=2), :]
    low = iota((c2 // 2, LANES), 1) < half
    tail[2 : 2 + c2 // 2, :] = jnp.where(low, odd, pltpu.roll(even, half, 1))
    start = 2 + c2 // 2
    low = iota((c2, LANES), 1) < half
    tail[start : start + c2, :] = jnp.where(
        low, pltpu.roll(third_s[0:c2, :], half, 1), pltpu.roll(third_s[1 : c2 + 1, :], half, 1)
    )
    tail[start + c2 : start + c2 + 1, :] = jnp.where(one, pltpu.roll(d_head, half, 1), 0.0)
    flat_hi[...] = tail[GROUP:, :]
    hi[0]()
    lax.fori_loop(0, steps // 2, first_grads, 0)
    hi[1]()
    lax.fori_loop(steps // 2, steps, first_grads, 0)
    hi[2]()

    g_first = [acc_first[k * c1 : (k + 1) * c1, :] for k in range(3)]
    weights = w_first[...].astype(F32)
    d_first = tap_cols[0] * g_first[0] + tap_cols[1] * g_first[1] + tap_cols[2] * g_first[2]
    tap_rows = [
        to_row(jnp.sum(weights * g, axis=1, keepdims=True), c1) for g in g_first
    ]
    first_lo[...] = d_first[:, 0:LANES]
    first_hi[:, 0 : feat - LANES] = d_first[:, LANES:feat]
    period = feat * GROUP // LANES
    groups = c1 // GROUP
    at = iota((groups, LANES), 1)
    flat_lo[...] = jnp.zeros_like(flat_lo)
    for j in range(period):
        chan, off = divmod(j * LANES, feat)
        lows = first_lo[pl.ds(chan, groups, stride=GROUP), :]
        highs = first_hi[pl.ds(chan, groups, stride=GROUP), :]
        value = pltpu.roll(highs, (-off) % LANES, 1)
        if off < LANES:
            shifted = pltpu.roll(lows, (-off) % LANES, 1) if off else lows
            value = jnp.where(at < LANES - off, shifted, value)
        if off + LANES > feat:
            after = first_lo[pl.ds(chan + 1, groups, stride=GROUP), :]
            value = jnp.where(at < feat - off, value, pltpu.roll(after, (feat - off) % LANES, 1))
        flat_lo[pl.ds(j, groups, stride=period), :] = value
    tail[0:1, :] = jnp.concatenate(tap_rows[0:2], axis=1)
    tail[1:2, :] = jnp.where(one, jnp.concatenate([tap_rows[2], tap_rows[2]], axis=1), tail[1:2, :])
    flat_lo[base : base + GROUP, :] = tail[0:GROUP, :]
    for phase in lo:
        phase()
    hi[3]()
    split = base + GROUP
    grads_out[0:split, :] = whole_lo[0:split, :]
    grads_out[split:, :] = whole_hi[...]


def on_device(
    n_tile, n_state,
    bands, block_slot, tile_counties, county_place, label, w_first, taps, w_second, w_third, w_head,
):
    feat, pixels = bands.shape[1:]
    c1, c2 = w_first.shape[0], w_second.shape[0]
    blocks = block_slot.shape[1]
    grads = c1 * feat + 3 * c1 + c2 * c1 + c2 * c2 + c2
    rows = pl.cdiv(grads, LANES)
    split = c1 * feat // LANES + GROUP
    share_lo = pl.cdiv(split, n_tile * GROUP) * GROUP
    share_hi = pl.cdiv(rows - split, n_tile * GROUP) * GROUP
    rows_lo, rows_hi = n_tile * share_lo, n_tile * share_hi
    steps = blocks // STEP_ROWS
    vmem = pl.BlockSpec(memory_space=pltpu.VMEM)
    dma = pltpu.SemaphoreType.DMA
    near = 2 * (REACH - 1)
    mean, out = pl.pallas_call(
        functools.partial(kernel, n_tile, n_state, share_lo, share_hi),
        out_shape=(
            jax.ShapeDtypeStruct(label.shape, F32),
            jax.ShapeDtypeStruct((split + rows_hi, LANES), F32),
        ),
        in_specs=[pl.BlockSpec(memory_space=pl.ANY)] + [vmem] * 9,
        out_specs=(vmem, vmem),
        scratch_shapes=[
            pltpu.VMEM((feat, pixels), BF16),
            pltpu.VMEM((c1, pixels), BF16),
            pltpu.VMEM((c2, pixels), BF16),
            pltpu.VMEM((c1, pixels), F32),
            pltpu.VMEM((c2, pixels), F32),
            pltpu.VMEM((c2, pixels), BF16),
            pltpu.VMEM((c2, pixels), BF16),
            pltpu.VMEM((3 * c1, pixels), BF16),
            pltpu.VMEM((blocks, LANES), F32),
            pltpu.VMEM((blocks, LANES), F32),
            pltpu.VMEM((c2, c1), BF16),
            pltpu.VMEM((c1, c2), BF16),
            pltpu.VMEM((c2, c2), BF16),
            pltpu.VMEM((c2, c2), BF16),
            pltpu.VMEM((c2, LANES), F32),
            pltpu.VMEM((3 * c1, feat), F32),
            pltpu.VMEM((c2, c1), F32),
            pltpu.VMEM((c2, c2), F32),
            pltpu.VMEM((2 * GROUP, c2), F32),
            pltpu.VMEM((c1, LANES), F32),
            pltpu.VMEM((c1, LANES), F32),
            pltpu.VMEM((c2 + GROUP, LANES), F32),
            pltpu.VMEM((c2 + GROUP, LANES), F32),
            pltpu.VMEM((GROUP + rows_hi, LANES), F32),
            pltpu.VMEM((GROUP, LANES), F32),
            pltpu.VMEM((near, GROUP, LANES), F32),
            pltpu.VMEM((rows_lo, LANES), F32),
            pltpu.VMEM((rows_hi, LANES), F32),
            pltpu.VMEM((n_tile - 1, share_lo, LANES), F32),
            pltpu.VMEM((n_tile - 1, share_hi, LANES), F32),
            pltpu.VMEM((n_state, share_lo, LANES), F32),
            pltpu.VMEM((n_state, share_hi, LANES), F32),
            pltpu.VMEM((rows_lo, LANES), F32),
            pltpu.VMEM((rows_hi, LANES), F32),
            dma((steps,)),
            dma((near,)),
            dma((near,)),
        ]
        + [
            dma((peers,))
            for peers in (n_tile - 1, n_tile - 1, n_state - 1, n_state - 1, n_tile - 1, n_tile - 1) * 2
        ],
        compiler_params=pltpu.CompilerParams(
            collective_id=0, has_side_effects=True, vmem_limit_bytes=56 * 2**20
        ),
    )(
        bands, block_slot, tile_counties, county_place, label,
        w_first, taps, w_second.T, w_third, w_head.reshape(1, -1),
    )
    return mean, out.reshape(-1)[:grads]


def solution(mesh):
    in_specs = (
        P("state", None, "tile"),
        P("state", "tile"),
        P("state", "tile"),
        P("state", None),
        P("state", "tile"),
        P(),
        P(),
        P(),
        P(),
        P(),
    )
    return jax.shard_map(
        functools.partial(on_device, mesh.shape["tile"], mesh.shape["state"]),
        mesh=mesh,
        in_specs=in_specs,
        out_specs=(P("state", "tile"), P()),
        check_vma=False,
    )
```

```python
import functools

import jax
import jax.numpy as jnp
from jax import lax
from jax.experimental import pallas as pl
from jax.experimental.pallas import tpu as pltpu
from jax.sharding import PartitionSpec as P

REACH = 4
LANES = 128
GROUP = 8
STEP_ROWS = 32
TICK_ROWS = 16
SUM_ROWS = 32
MESH = pl.DeviceIdType.MESH
F32 = jnp.float32
BF16 = jnp.bfloat16


def mm(left, right):
    return jnp.dot(left, right, preferred_element_type=F32)


def mm_last(left, right):
    return lax.dot_general(left, right, (((1,), (1,)), ((), ())), preferred_element_type=F32)


def iota(shape, dim):
    return lax.broadcasted_iota(jnp.int32, shape, dim)


def to_column(row, size):
    eye = iota((size, size), 0) == iota((size, size), 1)
    return jnp.sum(jnp.where(eye, row, 0.0), axis=1, keepdims=True)


def to_row(column, size):
    eye = iota((size, size), 0) == iota((size, size), 1)
    return jnp.sum(jnp.where(eye, column, 0.0), axis=0, keepdims=True)


def gate_parts(half):
    twice = jnp.tanh(half) + 1.0
    act = half * twice
    return act, twice + act * (2.0 - twice)


def kernel(
    n_tile, n_state, share_lo, share_hi,
    bands, slot_row, counties, table, label, w_first, taps, w_second, w_third, w_head,
    mean_out, grads_out,
    x_s, a1_s, a2_s, d1_s, d2_s, u3_s, u2_s, u1_s, slot_s, g_s, w2_s, w2t_s, w3_s, w3t_s, wh_s,
    acc_first, acc_second, acc_third, acc_head, first_lo, first_hi, second_s, third_s, tail,
    msg, msgs, flat_lo, flat_hi, parts_lo, parts_hi, zparts_lo, zparts_hi, whole_lo, whole_hi,
    x_sem, msg_send, msg_recv, *sum_sems,
):
    me = lax.axis_index("tile")
    my_state = lax.axis_index("state")
    c1, feat = w_first.shape
    c2 = w_second.shape[1]
    blocks = slot_row.shape[1]
    pixels = bands.shape[2]
    row_len = pixels // blocks
    cty_dev = label.shape[1]
    places = table.shape[1]
    slot_count = counties.shape[1]
    step_px = STEP_ROWS * row_len
    steps = pixels // step_px

    def band_copy(k):
        cols = pl.ds(pl.multiple_of(k * step_px, step_px), step_px)
        return pltpu.make_async_copy(bands.at[0, :, cols], x_s.at[:, cols], x_sem.at[k])

    for k in range(steps):
        band_copy(k).start()

    def tile_peer(by):
        return lax.rem(me + by + n_tile, n_tile)

    def state_peer(by):
        return lax.rem(my_state + by + n_state, n_state)

    barrier = pltpu.get_barrier_semaphore()
    for by in range(1, n_tile):
        pl.semaphore_signal(barrier, inc=1, device_id={"tile": tile_peer(by)}, device_id_type=MESH)
    for by in range(1, n_state):
        pl.semaphore_signal(
            barrier, inc=1, device_id={"state": state_peer(by)}, device_id_type=MESH
        )

    slots = slot_row[...].astype(F32)
    slot_s[...] = jnp.broadcast_to(to_column(slots, blocks), (blocks, LANES))
    half_second = w_second[...].astype(F32) * 0.5
    half_third = w_third[...].astype(F32) * 0.5
    w2t_s[...] = half_second.astype(BF16)
    w3_s[...] = half_third.astype(BF16)
    w2_s[...] = half_second.T.astype(BF16)
    w3t_s[...] = half_third.T.astype(BF16)
    head_row = w_head[...].astype(F32)
    wh_s[...] = jnp.broadcast_to(to_column(head_row, c2) * 0.5, (c2, LANES))
    tap_cols = [to_column(taps[k : k + 1, :], c1) for k in range(3)]
    lane = iota((c1, LANES), 1)
    tap_prev = jnp.where(lane == 0, 0.0, tap_cols[0] * 0.5)
    tap_here = jnp.broadcast_to(tap_cols[1] * 0.5, (c1, LANES))
    tap_next = jnp.where(lane == LANES - 1, 0.0, tap_cols[2] * 0.5)
    acc_first[...] = jnp.zeros_like(acc_first)
    acc_second[...] = jnp.zeros_like(acc_second)
    acc_third[...] = jnp.zeros_like(acc_third)
    acc_head[...] = jnp.zeros_like(acc_head)
    slot_ids = iota((2 * GROUP, LANES), 0).astype(F32)

    def row_cols(j):
        return slice(j * row_len, (j + 1) * row_len)

    ticks = STEP_ROWS // TICK_ROWS
    tick_px = TICK_ROWS * row_len

    def columns(step, tick, j=None):
        first = step * step_px + tick * tick_px + (0 if j is None else j * row_len)
        size = tick_px if j is None else row_len
        return pl.ds(pl.multiple_of(first, row_len), size)

    def skewed(stages):
        held = [None] * len(stages)
        for now in range(ticks + len(stages) - 1):
            for n in reversed(range(len(stages))):
                tick = now - n
                if 0 <= tick < ticks:
                    held[n] = stages[n](tick, held[n - 1] if n else None)

    def halves():
        return [slice(r, r + c1) for r in range(0, c2, c1)]

    def forward(step, carry):
        band_copy(step).wait()
        head = [acc_head[...]]

        def stage_one(tick, _):
            return mm(w_first[...], x_s[:, columns(step, tick)])

        def stage_two(tick, h1):
            tiles = []
            for j in range(TICK_ROWS):
                h = h1[:, row_cols(j)]
                s1 = (
                    tap_prev * pltpu.roll(h, 1, 1)
                    + tap_here * h
                    + tap_next * pltpu.roll(h, LANES - 1, 1)
                )
                act, d1_s[:, columns(step, tick, j)] = gate_parts(s1)
                act = act.astype(BF16)
                a1_s[:, columns(step, tick, j)] = act
                tiles.append(act)
            return mm(w2_s[...], jnp.concatenate(tiles, axis=1))

        def stage_three(tick, h2):
            tiles = []
            for j in range(TICK_ROWS):
                parts = []
                for part in halves():
                    act, d2_s[part, columns(step, tick, j)] = gate_parts(h2[part, row_cols(j)])
                    act = act.astype(BF16)
                    a2_s[part, columns(step, tick, j)] = act
                    parts.append(act)
                tiles.append(jnp.concatenate(parts, axis=0))
            tiles = jnp.concatenate(tiles, axis=1)
            return mm(w3_s[...], tiles), tiles

        def stage_four(tick, before):
            h3, a2 = before
            tiles, members = [], []
            for j in range(TICK_ROWS):
                parts = []
                for part in halves():
                    act, d3 = gate_parts(h3[part, row_cols(j)])
                    u3_s[part, columns(step, tick, j)] = (wh_s[part, :] * d3).astype(BF16)
                    parts.append((act + a2[part, row_cols(j)].astype(F32)).astype(BF16))
                tiles.append(jnp.concatenate(parts, axis=0))
                row = slot_s[pl.ds(step * STEP_ROWS + tick * TICK_ROWS + j, 1), :]
                members.append((row == slot_ids).astype(F32).astype(BF16))
            head[0] = head[0] + mm_last(
                jnp.concatenate(members, axis=1), jnp.concatenate(tiles, axis=1)
            )

        skewed([stage_one, stage_two, stage_three, stage_four])
        acc_head[...] = head[0]
        return carry

    lax.fori_loop(0, steps, forward, 0)

    head_sums = acc_head[0:GROUP, :]
    slot_sums = jnp.sum(head_sums * head_row, axis=1, keepdims=True)
    in_slot = (slots == slot_ids[0:GROUP, :]).astype(F32)
    slot_counts = jnp.sum(in_slot, axis=1, keepdims=True) * float(row_len)
    county = to_column(counties[...].astype(F32), slot_count)
    hits = county == iota((slot_count, places), 1).astype(F32)
    place = jnp.sum(jnp.where(hits, table[...].astype(F32), 0.0), axis=1, keepdims=True)
    place = place - (me * cty_dev).astype(F32)
    place = jnp.where(place < 0.0, place + float(places), place)
    pick = (place == iota((slot_count, LANES), 1).astype(F32)).astype(F32)
    msg[...] = jnp.zeros_like(msg)
    msg[0:1, :] = jnp.sum(pick * slot_sums, axis=0, keepdims=True)
    msg[1:2, :] = jnp.sum(pick * slot_counts, axis=0, keepdims=True)
    msg[2:3, 0:cty_dev] = label[...].astype(F32)

    pl.semaphore_wait(barrier, n_tile - 1 + n_state - 1)
    offsets = [by for by in range(1 - REACH, REACH) if by]
    copies = []
    for n, by in enumerate(offsets):
        copies.append(
            pltpu.make_async_remote_copy(
                src_ref=msg,
                dst_ref=msgs.at[n],
                send_sem=msg_send.at[n],
                recv_sem=msg_recv.at[n],
                device_id={"tile": tile_peer(by)},
                device_id_type=MESH,
            )
        )
        copies[-1].start()

    def backward(step, carry):
        def stage_one(tick, _):
            return mm(w3t_s[...], u3_s[:, columns(step, tick)])

        def stage_two(tick, d_a2):
            tiles = []
            for j in range(TICK_ROWS):
                parts = []
                for part in halves():
                    d_h2 = (d_a2[part, row_cols(j)] + wh_s[part, :]) * d2_s[part, columns(step, tick, j)]
                    d_h2 = d_h2.astype(BF16)
                    u2_s[part, columns(step, tick, j)] = d_h2
                    parts.append(d_h2)
                tiles.append(jnp.concatenate(parts, axis=0))
            return mm(w2t_s[...], jnp.concatenate(tiles, axis=1))

        def stage_three(tick, d_a1):
            for j in range(TICK_ROWS):
                cols = columns(step, tick, j)
                d = d_a1[:, row_cols(j)] * d1_s[:, cols]
                u1_s[0:c1, cols] = jnp.where(
                    lane == LANES - 1, 0.0, pltpu.roll(d, LANES - 1, 1)
                ).astype(BF16)
                u1_s[c1 : 2 * c1, cols] = d.astype(BF16)
                u1_s[2 * c1 : 3 * c1, cols] = jnp.where(lane == 0, 0.0, pltpu.roll(d, 1, 1)).astype(
                    BF16
                )

        skewed([stage_one, stage_two, stage_three])
        return carry

    lax.fori_loop(0, steps, backward, 0)

    total = msg[...]
    for n, by in enumerate(offsets):
        copies[n].wait_recv()
        total = total + pltpu.roll(msgs[n], (-by * cty_dev) % LANES, 1)
    for copy in copies:
        copy.wait_send()
    sums, counts, target = total[0:1, :], total[1:2, :], total[2:3, :] * 0.01
    denom = jnp.maximum(counts, 1.0)
    mean = sums / denom
    mean_out[...] = mean[:, 0:cty_dev]
    adjoint = jnp.where(
        counts > 0.5, 2.0 * (mean - target) / (float(n_tile * n_state) * denom), 0.0
    )
    slot_g = jnp.sum(jnp.where(pick > 0.5, adjoint, 0.0), axis=1, keepdims=True)
    slot_g = slot_g.astype(BF16).astype(F32)
    all_slots = slot_s[...]
    g_rows = jnp.zeros((blocks, LANES), F32)
    for s in range(slot_count):
        g_rows = jnp.where(all_slots == float(s), slot_g[s : s + 1, 0:1], g_rows)
    g_s[...] = g_rows

    def scaled(field, first):
        tiles = []
        for j in range(SUM_ROWS):
            row = jnp.broadcast_to(g_s[pl.ds(first + j, 1), :], (2 * GROUP, LANES)).astype(BF16)
            tile = jnp.concatenate([row] * (field.shape[0] // (2 * GROUP)), axis=0)
            cols = pl.ds(pl.multiple_of((first + j) * row_len, row_len), row_len)
            tiles.append(field[:, cols] * tile)
        return jnp.concatenate(tiles, axis=1)

    def chunks(step):
        for n in range(STEP_ROWS // SUM_ROWS):
            first = step * STEP_ROWS + n * SUM_ROWS
            px = SUM_ROWS * row_len
            yield first, pl.ds(pl.multiple_of(first * row_len, px), px)

    def deep_grads(step, carry):
        third, second = acc_third[...], acc_second[...]
        for first, cols in chunks(step):
            third = third + mm_last(scaled(u3_s, first), a2_s[:, cols])
            second = second + mm_last(scaled(u2_s, first), a1_s[:, cols])
        acc_third[...] = third
        acc_second[...] = second
        return carry

    def first_grads(step, carry):
        for first, cols in chunks(step):
            acc_first[...] += mm_last(scaled(u1_s, first), x_s[:, cols])
        return carry

    def summing(share, flat, parts, zparts, whole, part_send, part_recv, z_send, z_recv, all_send, all_recv):
        def share_of(index):
            return pl.ds(pl.multiple_of(index * share, share), share)

        scatter, across, gather = [], [], []
        for by in range(1, n_tile):
            peer = tile_peer(by)
            where = {"tile": peer}
            scatter.append(
                pltpu.make_async_remote_copy(
                    src_ref=flat.at[share_of(peer)],
                    dst_ref=parts.at[by - 1],
                    send_sem=part_send.at[by - 1],
                    recv_sem=part_recv.at[by - 1],
                    device_id=where,
                    device_id_type=MESH,
                )
            )
            gather.append(
                pltpu.make_async_remote_copy(
                    src_ref=whole.at[share_of(me)],
                    dst_ref=whole.at[share_of(me)],
                    send_sem=all_send.at[by - 1],
                    recv_sem=all_recv.at[by - 1],
                    device_id=where,
                    device_id_type=MESH,
                )
            )
        for by in range(1, n_state):
            across.append(
                pltpu.make_async_remote_copy(
                    src_ref=zparts.at[my_state],
                    dst_ref=zparts.at[my_state],
                    send_sem=z_send.at[by - 1],
                    recv_sem=z_recv.at[by - 1],
                    device_id={"state": state_peer(by)},
                    device_id_type=MESH,
                )
            )

        def first():
            for copy in scatter:
                copy.start()

        def second():
            piece = flat[share_of(me), :]
            for n, copy in enumerate(scatter):
                copy.wait_recv()
                piece = piece + parts[n]
            zparts[my_state] = piece
            for copy in across:
                copy.start()

        def third():
            for copy in across:
                copy.wait_recv()
            piece = zparts[0]
            for s in range(1, n_state):
                piece = piece + zparts[s]
            whole[share_of(me), :] = piece
            for copy in gather:
                copy.start()

        def last():
            for copy in gather:
                copy.wait_recv()
            for copy in scatter + across + gather:
                copy.wait_send()

        return first, second, third, last

    lo = summing(share_lo, flat_lo, parts_lo, zparts_lo, whole_lo, *sum_sems[0:6])
    hi = summing(share_hi, flat_hi, parts_hi, zparts_hi, whole_hi, *sum_sems[6:12])

    lax.fori_loop(0, steps, deep_grads, 0)

    base = c1 * feat // LANES
    half = LANES // 2
    d_head = jnp.sum(head_sums * slot_g, axis=0, keepdims=True)
    second_s[...] = jnp.zeros_like(second_s)
    second_s[0:c2, 0:half] = acc_second[...]
    third_s[0:c2, :] = acc_third[...]
    third_s[c2 : c2 + 1, :] = d_head
    second_s[c2 : c2 + 1, :] = third_s[0:1, :]
    one = iota((1, LANES), 1) < half
    tail[...] = jnp.zeros_like(tail)
    tail[1:2, :] = pltpu.roll(second_s[0:1, :], half, 1)
    odd = second_s[pl.ds(1, c2 // 2, stride=2), :]
    even = second_s[pl.ds(2, c2 // 2, stride=2), :]
    low = iota((c2 // 2, LANES), 1) < half
    tail[2 : 2 + c2 // 2, :] = jnp.where(low, odd, pltpu.roll(even, half, 1))
    start = 2 + c2 // 2
    low = iota((c2, LANES), 1) < half
    tail[start : start + c2, :] = jnp.where(
        low, pltpu.roll(third_s[0:c2, :], half, 1), pltpu.roll(third_s[1 : c2 + 1, :], half, 1)
    )
    tail[start + c2 : start + c2 + 1, :] = jnp.where(one, pltpu.roll(d_head, half, 1), 0.0)
    flat_hi[...] = tail[GROUP:, :]
    hi[0]()
    lax.fori_loop(0, steps // 2, first_grads, 0)
    hi[1]()
    lax.fori_loop(steps // 2, steps, first_grads, 0)
    hi[2]()

    g_first = [acc_first[k * c1 : (k + 1) * c1, :] for k in range(3)]
    weights = w_first[...].astype(F32)
    d_first = tap_cols[0] * g_first[0] + tap_cols[1] * g_first[1] + tap_cols[2] * g_first[2]
    tap_rows = [
        to_row(jnp.sum(weights * g, axis=1, keepdims=True), c1) for g in g_first
    ]
    first_lo[...] = d_first[:, 0:LANES]
    first_hi[:, 0 : feat - LANES] = d_first[:, LANES:feat]
    period = feat * GROUP // LANES
    groups = c1 // GROUP
    at = iota((groups, LANES), 1)
    flat_lo[...] = jnp.zeros_like(flat_lo)
    for j in range(period):
        chan, off = divmod(j * LANES, feat)
        lows = first_lo[pl.ds(chan, groups, stride=GROUP), :]
        highs = first_hi[pl.ds(chan, groups, stride=GROUP), :]
        value = pltpu.roll(highs, (-off) % LANES, 1)
        if off < LANES:
            shifted = pltpu.roll(lows, (-off) % LANES, 1) if off else lows
            value = jnp.where(at < LANES - off, shifted, value)
        if off + LANES > feat:
            after = first_lo[pl.ds(chan + 1, groups, stride=GROUP), :]
            value = jnp.where(at < feat - off, value, pltpu.roll(after, (feat - off) % LANES, 1))
        flat_lo[pl.ds(j, groups, stride=period), :] = value
    tail[0:1, :] = jnp.concatenate(tap_rows[0:2], axis=1)
    tail[1:2, :] = jnp.where(one, jnp.concatenate([tap_rows[2], tap_rows[2]], axis=1), tail[1:2, :])
    flat_lo[base : base + GROUP, :] = tail[0:GROUP, :]
    for phase in lo:
        phase()
    hi[3]()
    split = base + GROUP
    grads_out[0:split, :] = whole_lo[0:split, :]
    grads_out[split:, :] = whole_hi[...]


def on_device(
    n_tile, n_state,
    bands, block_slot, tile_counties, county_place, label, w_first, taps, w_second, w_third, w_head,
):
    feat, pixels = bands.shape[1:]
    c1, c2 = w_first.shape[0], w_second.shape[0]
    blocks = block_slot.shape[1]
    grads = c1 * feat + 3 * c1 + c2 * c1 + c2 * c2 + c2
    rows = pl.cdiv(grads, LANES)
    split = c1 * feat // LANES + GROUP
    share_lo = pl.cdiv(split, n_tile * GROUP) * GROUP
    share_hi = pl.cdiv(rows - split, n_tile * GROUP) * GROUP
    rows_lo, rows_hi = n_tile * share_lo, n_tile * share_hi
    steps = blocks // STEP_ROWS
    vmem = pl.BlockSpec(memory_space=pltpu.VMEM)
    dma = pltpu.SemaphoreType.DMA
    near = 2 * (REACH - 1)
    mean, out = pl.pallas_call(
        functools.partial(kernel, n_tile, n_state, share_lo, share_hi),
        out_shape=(
            jax.ShapeDtypeStruct(label.shape, F32),
            jax.ShapeDtypeStruct((split + rows_hi, LANES), F32),
        ),
        in_specs=[pl.BlockSpec(memory_space=pl.ANY)] + [vmem] * 9,
        out_specs=(vmem, vmem),
        scratch_shapes=[
            pltpu.VMEM((feat, pixels), BF16),
            pltpu.VMEM((c1, pixels), BF16),
            pltpu.VMEM((c2, pixels), BF16),
            pltpu.VMEM((c1, pixels), F32),
            pltpu.VMEM((c2, pixels), F32),
            pltpu.VMEM((c2, pixels), BF16),
            pltpu.VMEM((c2, pixels), BF16),
            pltpu.VMEM((3 * c1, pixels), BF16),
            pltpu.VMEM((blocks, LANES), F32),
            pltpu.VMEM((blocks, LANES), F32),
            pltpu.VMEM((c2, c1), BF16),
            pltpu.VMEM((c1, c2), BF16),
            pltpu.VMEM((c2, c2), BF16),
            pltpu.VMEM((c2, c2), BF16),
            pltpu.VMEM((c2, LANES), F32),
            pltpu.VMEM((3 * c1, feat), F32),
            pltpu.VMEM((c2, c1), F32),
            pltpu.VMEM((c2, c2), F32),
            pltpu.VMEM((2 * GROUP, c2), F32),
            pltpu.VMEM((c1, LANES), F32),
            pltpu.VMEM((c1, LANES), F32),
            pltpu.VMEM((c2 + GROUP, LANES), F32),
            pltpu.VMEM((c2 + GROUP, LANES), F32),
            pltpu.VMEM((GROUP + rows_hi, LANES), F32),
            pltpu.VMEM((GROUP, LANES), F32),
            pltpu.VMEM((near, GROUP, LANES), F32),
            pltpu.VMEM((rows_lo, LANES), F32),
            pltpu.VMEM((rows_hi, LANES), F32),
            pltpu.VMEM((n_tile - 1, share_lo, LANES), F32),
            pltpu.VMEM((n_tile - 1, share_hi, LANES), F32),
            pltpu.VMEM((n_state, share_lo, LANES), F32),
            pltpu.VMEM((n_state, share_hi, LANES), F32),
            pltpu.VMEM((rows_lo, LANES), F32),
            pltpu.VMEM((rows_hi, LANES), F32),
            dma((steps,)),
            dma((near,)),
            dma((near,)),
        ]
        + [
            dma((peers,))
            for peers in (n_tile - 1, n_tile - 1, n_state - 1, n_state - 1, n_tile - 1, n_tile - 1) * 2
        ],
        compiler_params=pltpu.CompilerParams(
            collective_id=0, has_side_effects=True, vmem_limit_bytes=56 * 2**20
        ),
    )(
        bands, block_slot, tile_counties, county_place, label,
        w_first, taps, w_second.T, w_third, w_head.reshape(1, -1),
    )
    return mean, out.reshape(-1)[:grads]


def solution(mesh):
    in_specs = (
        P("state", None, "tile"),
        P("state", "tile"),
        P("state", "tile"),
        P("state", None),
        P("state", "tile"),
        P(),
        P(),
        P(),
        P(),
        P(),
    )
    return jax.shard_map(
        functools.partial(on_device, mesh.shape["tile"], mesh.shape["state"]),
        mesh=mesh,
        in_specs=in_specs,
        out_specs=(P("state", "tile"), P()),
        check_vma=False,
    )
```

```python
import functools

import jax
import jax.numpy as jnp
from jax import lax
from jax.experimental import pallas as pl
from jax.experimental.pallas import tpu as pltpu
from jax.sharding import PartitionSpec as P

REACH = 4
LANES = 128
GROUP = 8
STEP_ROWS = 32
DMA_STEPS = 4
MESH = pl.DeviceIdType.MESH
F32 = jnp.float32
BF16 = jnp.bfloat16


def mm(left, right):
    return jnp.dot(left, right, preferred_element_type=F32)


def mm_last(left, right):
    return lax.dot_general(left, right, (((1,), (1,)), ((), ())), preferred_element_type=F32)


def iota(shape, dim):
    return lax.broadcasted_iota(jnp.int32, shape, dim)


def to_column(row, size):
    eye = iota((size, size), 0) == iota((size, size), 1)
    return jnp.sum(jnp.where(eye, row, 0.0), axis=1, keepdims=True)


def to_row(column, size):
    eye = iota((size, size), 0) == iota((size, size), 1)
    return jnp.sum(jnp.where(eye, column, 0.0), axis=0, keepdims=True)


def gate_parts(half):
    twice = jnp.tanh(half) + 1.0
    act = half * twice
    return act, twice + act * (2.0 - twice)


def kernel(
    n_tile, n_state, share,
    bands, slot_row, counties, table, label, w_first, taps, w_second, w_third, w_head,
    mean_out, grads_out,
    x_s, a1_s, a2_s, d1_s, d2_s, d3_s, slot_s, g_s, w2_s, w2t_s, w3_s, w3t_s, wh_s,
    acc_first, acc_second, acc_third, acc_head, first_lo, first_hi, second_s, third_s,
    flat, msg, msgs, parts, zparts, whole,
    x_sem, msg_send, msg_recv, part_send, part_recv, z_send, z_recv, all_send, all_recv,
):
    me = lax.axis_index("tile")
    my_state = lax.axis_index("state")
    c1, feat = w_first.shape
    c2 = w_second.shape[1]
    blocks = slot_row.shape[1]
    pixels = bands.shape[2]
    row_len = pixels // blocks
    cty_dev = label.shape[1]
    places = table.shape[1]
    slot_count = counties.shape[1]
    step_px = STEP_ROWS * row_len
    dma_px = pixels // DMA_STEPS
    steps_per_dma = dma_px // step_px

    def band_copy(k):
        cols = pl.ds(pl.multiple_of(k * dma_px, dma_px), dma_px)
        return pltpu.make_async_copy(bands.at[0, :, cols], x_s.at[:, cols], x_sem.at[k])

    for k in range(DMA_STEPS):
        band_copy(k).start()

    def tile_peer(by):
        return lax.rem(me + by + n_tile, n_tile)

    def state_peer(by):
        return lax.rem(my_state + by + n_state, n_state)

    barrier = pltpu.get_barrier_semaphore()
    for by in range(1, n_tile):
        pl.semaphore_signal(barrier, inc=1, device_id={"tile": tile_peer(by)}, device_id_type=MESH)
    for by in range(1, n_state):
        pl.semaphore_signal(
            barrier, inc=1, device_id={"state": state_peer(by)}, device_id_type=MESH
        )

    slots = slot_row[...].astype(F32)
    slot_s[...] = jnp.broadcast_to(to_column(slots, blocks), (blocks, LANES))
    half_second = w_second[...].astype(F32) * 0.5
    half_third = w_third[...].astype(F32) * 0.5
    w2t_s[...] = half_second.astype(BF16)
    w3_s[...] = half_third.astype(BF16)
    w2_s[...] = half_second.T.astype(BF16)
    w3t_s[...] = half_third.T.astype(BF16)
    head_row = w_head[...].astype(F32)
    wh_s[...] = jnp.broadcast_to(to_column(head_row, c2) * 0.5, (c2, LANES))
    tap_cols = [to_column(taps[k : k + 1, :], c1) for k in range(3)]
    lane = iota((c1, LANES), 1)
    tap_prev = jnp.where(lane == 0, 0.0, tap_cols[0] * 0.5)
    tap_here = jnp.broadcast_to(tap_cols[1] * 0.5, (c1, LANES))
    tap_next = jnp.where(lane == LANES - 1, 0.0, tap_cols[2] * 0.5)
    acc_first[...] = jnp.zeros_like(acc_first)
    acc_second[...] = jnp.zeros_like(acc_second)
    acc_third[...] = jnp.zeros_like(acc_third)
    acc_head[...] = jnp.zeros_like(acc_head)
    slot_ids = iota((2 * GROUP, LANES), 0).astype(F32)

    def row_cols(j):
        return slice(j * row_len, (j + 1) * row_len)

    def forward(step):
        cols = pl.ds(pl.multiple_of(step * step_px, step_px), step_px)
        h1 = mm(w_first[...], x_s[:, cols])
        s1 = []
        for j in range(STEP_ROWS):
            h = h1[:, row_cols(j)]
            s1.append(
                tap_prev * pltpu.roll(h, 1, 1)
                + tap_here * h
                + tap_next * pltpu.roll(h, LANES - 1, 1)
            )
        a1, d1 = gate_parts(jnp.concatenate(s1, axis=1))
        d1_s[:, cols] = d1
        a1 = a1.astype(BF16)
        a1_s[:, cols] = a1
        a2, d2 = gate_parts(mm(w2_s[...], a1))
        d2_s[:, cols] = d2
        a2 = a2.astype(BF16)
        a2_s[:, cols] = a2
        a3, d3 = gate_parts(mm(w3_s[...], a2))
        d3_s[:, cols] = d3
        a3 = (a3 + a2.astype(F32)).astype(BF16)
        member = jnp.concatenate(
            [
                (slot_s[pl.ds(step * STEP_ROWS + j, 1), :] == slot_ids).astype(F32)
                for j in range(STEP_ROWS)
            ],
            axis=1,
        ).astype(BF16)
        acc_head[...] += mm_last(member, a3)

    def forward_dma(k, carry):
        band_copy(k).wait()

        def inner(i, c):
            forward(k * steps_per_dma + i)
            return c

        return lax.fori_loop(0, steps_per_dma, inner, carry)

    lax.fori_loop(0, DMA_STEPS, forward_dma, 0)

    head_sums = acc_head[0:GROUP, :]
    slot_sums = jnp.sum(head_sums * head_row, axis=1, keepdims=True)
    in_slot = (slots == slot_ids[0:GROUP, :]).astype(F32)
    slot_counts = jnp.sum(in_slot, axis=1, keepdims=True) * float(row_len)
    county = to_column(counties[...].astype(F32), slot_count)
    hits = county == iota((slot_count, places), 1).astype(F32)
    place = jnp.sum(jnp.where(hits, table[...].astype(F32), 0.0), axis=1, keepdims=True)
    place = place - (me * cty_dev).astype(F32)
    place = jnp.where(place < 0.0, place + float(places), place)
    pick = (place == iota((slot_count, LANES), 1).astype(F32)).astype(F32)
    msg[...] = jnp.zeros_like(msg)
    msg[0:1, :] = jnp.sum(pick * slot_sums, axis=0, keepdims=True)
    msg[1:2, :] = jnp.sum(pick * slot_counts, axis=0, keepdims=True)
    msg[2:3, 0:cty_dev] = label[...].astype(F32)

    pl.semaphore_wait(barrier, n_tile - 1 + n_state - 1)
    offsets = [by for by in range(1 - REACH, REACH) if by]
    copies = []
    for n, by in enumerate(offsets):
        copies.append(
            pltpu.make_async_remote_copy(
                src_ref=msg,
                dst_ref=msgs.at[n],
                send_sem=msg_send.at[n],
                recv_sem=msg_recv.at[n],
                device_id={"tile": tile_peer(by)},
                device_id_type=MESH,
            )
        )
        copies[-1].start()
    total = msg[...]
    for n, by in enumerate(offsets):
        copies[n].wait_recv()
        total = total + pltpu.roll(msgs[n], (-by * cty_dev) % LANES, 1)
    for copy in copies:
        copy.wait_send()
    sums, counts, target = total[0:1, :], total[1:2, :], total[2:3, :] * 0.01
    denom = jnp.maximum(counts, 1.0)
    mean = sums / denom
    mean_out[...] = mean[:, 0:cty_dev]
    adjoint = jnp.where(
        counts > 0.5, 2.0 * (mean - target) / (float(n_tile * n_state) * denom), 0.0
    )
    slot_g = jnp.sum(jnp.where(pick > 0.5, adjoint, 0.0), axis=1, keepdims=True)
    slot_g = slot_g.astype(BF16).astype(F32)
    all_slots = slot_s[...]
    g_rows = jnp.zeros((blocks, LANES), F32)
    for s in range(slot_count):
        g_rows = jnp.where(all_slots == float(s), slot_g[s : s + 1, 0:1], g_rows)
    g_s[...] = g_rows

    def backward(step, carry):
        cols = pl.ds(pl.multiple_of(step * step_px, step_px), step_px)
        x = x_s[:, cols]
        a1 = a1_s[:, cols]
        a2 = a2_s[:, cols]
        wh = wh_s[...]
        d_a3 = jnp.concatenate(
            [wh * g_s[pl.ds(step * STEP_ROWS + j, 1), :] for j in range(STEP_ROWS)], axis=1
        )
        d_h3 = (d_a3 * d3_s[:, cols]).astype(BF16)
        acc_third[...] += mm_last(d_h3, a2)
        d_h2 = ((mm(w3t_s[...], d_h3) + d_a3) * d2_s[:, cols]).astype(BF16)
        acc_second[...] += mm_last(d_h2, a1)
        d_s1 = mm(w2t_s[...], d_h2) * d1_s[:, cols]
        left, right = [], []
        for j in range(STEP_ROWS):
            d = d_s1[:, row_cols(j)]
            left.append(jnp.where(lane == LANES - 1, 0.0, pltpu.roll(d, LANES - 1, 1)))
            right.append(jnp.where(lane == 0, 0.0, pltpu.roll(d, 1, 1)))
        shifted = jnp.concatenate(
            [jnp.concatenate(left, axis=1), d_s1, jnp.concatenate(right, axis=1)], axis=0
        ).astype(BF16)
        acc_first[...] += mm_last(shifted, x)
        return carry

    lax.fori_loop(0, pixels // step_px, backward, 0)

    g_first = [acc_first[k * c1 : (k + 1) * c1, :] for k in range(3)]
    weights = w_first[...].astype(F32)
    d_first = tap_cols[0] * g_first[0] + tap_cols[1] * g_first[1] + tap_cols[2] * g_first[2]
    tap_rows = [
        to_row(jnp.sum(weights * g, axis=1, keepdims=True), c1) for g in g_first
    ]
    d_head = jnp.sum(head_sums * slot_g, axis=0, keepdims=True)
    first_lo[...] = d_first[:, 0:LANES]
    first_hi[:, 0 : feat - LANES] = d_first[:, LANES:feat]
    flat[...] = jnp.zeros_like(flat)
    period = feat * GROUP // LANES
    groups = c1 // GROUP
    at = iota((groups, LANES), 1)
    for j in range(period):
        chan, off = divmod(j * LANES, feat)
        lo = first_lo[pl.ds(chan, groups, stride=GROUP), :]
        hi = first_hi[pl.ds(chan, groups, stride=GROUP), :]
        value = pltpu.roll(hi, (-off) % LANES, 1)
        if off < LANES:
            lo_part = pltpu.roll(lo, (-off) % LANES, 1) if off else lo
            value = jnp.where(at < LANES - off, lo_part, value)
        if off + LANES > feat:
            after = first_lo[pl.ds(chan + 1, groups, stride=GROUP), :]
            value = jnp.where(at < feat - off, value, pltpu.roll(after, (feat - off) % LANES, 1))
        flat[pl.ds(j, groups, stride=period), :] = value
    base = c1 * feat // LANES
    half = LANES // 2
    second_s[...] = jnp.zeros_like(second_s)
    second_s[0:c2, 0:half] = acc_second[...]
    third_s[0:c2, :] = acc_third[...]
    third_s[c2 : c2 + 1, :] = d_head
    second_s[c2 : c2 + 1, :] = third_s[0:1, :]
    one = iota((1, LANES), 1) < half
    flat[base : base + 1, :] = jnp.concatenate(tap_rows[0:2], axis=1)
    flat[base + 1 : base + 2, :] = jnp.where(
        one,
        jnp.concatenate([tap_rows[2], tap_rows[2]], axis=1),
        pltpu.roll(second_s[0:1, :], half, 1),
    )
    odd = second_s[pl.ds(1, c2 // 2, stride=2), :]
    even = second_s[pl.ds(2, c2 // 2, stride=2), :]
    low = iota((c2 // 2, LANES), 1) < half
    flat[base + 2 : base + 2 + c2 // 2, :] = jnp.where(low, odd, pltpu.roll(even, half, 1))
    start = base + 2 + c2 // 2
    low = iota((c2, LANES), 1) < half
    flat[start : start + c2, :] = jnp.where(
        low, pltpu.roll(third_s[0:c2, :], half, 1), pltpu.roll(third_s[1 : c2 + 1, :], half, 1)
    )
    flat[start + c2 : start + c2 + 1, :] = jnp.where(one, pltpu.roll(d_head, half, 1), 0.0)

    def share_of(index):
        return pl.ds(pl.multiple_of(index * share, share), share)

    copies = []
    for by in range(1, n_tile):
        peer = tile_peer(by)
        copies.append(
            pltpu.make_async_remote_copy(
                src_ref=flat.at[share_of(peer)],
                dst_ref=parts.at[by - 1],
                send_sem=part_send.at[by - 1],
                recv_sem=part_recv.at[by - 1],
                device_id={"tile": peer},
                device_id_type=MESH,
            )
        )
        copies[-1].start()
    piece = flat[share_of(me), :]
    for n, copy in enumerate(copies):
        copy.wait_recv()
        piece = piece + parts[n]
    zparts[my_state] = piece
    zcopies = []
    for by in range(1, n_state):
        zcopies.append(
            pltpu.make_async_remote_copy(
                src_ref=zparts.at[my_state],
                dst_ref=zparts.at[my_state],
                send_sem=z_send.at[by - 1],
                recv_sem=z_recv.at[by - 1],
                device_id={"state": state_peer(by)},
                device_id_type=MESH,
            )
        )
        zcopies[-1].start()
    for copy in zcopies:
        copy.wait_recv()
    piece = zparts[0]
    for s in range(1, n_state):
        piece = piece + zparts[s]
    whole[share_of(me), :] = piece
    acopies = []
    for by in range(1, n_tile):
        acopies.append(
            pltpu.make_async_remote_copy(
                src_ref=whole.at[share_of(me)],
                dst_ref=whole.at[share_of(me)],
                send_sem=all_send.at[by - 1],
                recv_sem=all_recv.at[by - 1],
                device_id={"tile": tile_peer(by)},
                device_id_type=MESH,
            )
        )
        acopies[-1].start()
    for copy in copies:
        copy.wait_send()
    for copy in zcopies:
        copy.wait_send()
    for copy in acopies:
        copy.wait_recv()
    for copy in acopies:
        copy.wait_send()
    grads_out[...] = whole[...]


def on_device(
    n_tile, n_state,
    bands, block_slot, tile_counties, county_place, label, w_first, taps, w_second, w_third, w_head,
):
    feat, pixels = bands.shape[1:]
    c1, c2 = w_first.shape[0], w_second.shape[0]
    blocks = block_slot.shape[1]
    grads = c1 * feat + 3 * c1 + c2 * c1 + c2 * c2 + c2
    rows = pl.cdiv(grads, LANES)
    share = pl.cdiv(rows, n_tile * GROUP) * GROUP
    vmem = pl.BlockSpec(memory_space=pltpu.VMEM)
    dma = pltpu.SemaphoreType.DMA
    near = 2 * (REACH - 1)
    mean, out = pl.pallas_call(
        functools.partial(kernel, n_tile, n_state, share),
        out_shape=(
            jax.ShapeDtypeStruct(label.shape, F32),
            jax.ShapeDtypeStruct((n_tile * share, LANES), F32),
        ),
        in_specs=[pl.BlockSpec(memory_space=pl.ANY)] + [vmem] * 9,
        out_specs=(vmem, vmem),
        scratch_shapes=[
            pltpu.VMEM((feat, pixels), BF16),
            pltpu.VMEM((c1, pixels), BF16),
            pltpu.VMEM((c2, pixels), BF16),
            pltpu.VMEM((c1, pixels), F32),
            pltpu.VMEM((c2, pixels), F32),
            pltpu.VMEM((c2, pixels), F32),
            pltpu.VMEM((blocks, LANES), F32),
            pltpu.VMEM((blocks, LANES), F32),
            pltpu.VMEM((c2, c1), BF16),
            pltpu.VMEM((c1, c2), BF16),
            pltpu.VMEM((c2, c2), BF16),
            pltpu.VMEM((c2, c2), BF16),
            pltpu.VMEM((c2, LANES), F32),
            pltpu.VMEM((3 * c1, feat), F32),
            pltpu.VMEM((c2, c1), F32),
            pltpu.VMEM((c2, c2), F32),
            pltpu.VMEM((2 * GROUP, c2), F32),
            pltpu.VMEM((c1, LANES), F32),
            pltpu.VMEM((c1, LANES), F32),
            pltpu.VMEM((c2 + GROUP, LANES), F32),
            pltpu.VMEM((c2 + GROUP, LANES), F32),
            pltpu.VMEM((n_tile * share, LANES), F32),
            pltpu.VMEM((GROUP, LANES), F32),
            pltpu.VMEM((near, GROUP, LANES), F32),
            pltpu.VMEM((n_tile - 1, share, LANES), F32),
            pltpu.VMEM((n_state, share, LANES), F32),
            pltpu.VMEM((n_tile * share, LANES), F32),
            dma((DMA_STEPS,)),
            dma((near,)),
            dma((near,)),
            dma((n_tile - 1,)),
            dma((n_tile - 1,)),
            dma((n_state - 1,)),
            dma((n_state - 1,)),
            dma((n_tile - 1,)),
            dma((n_tile - 1,)),
        ],
        compiler_params=pltpu.CompilerParams(
            collective_id=0, has_side_effects=True, vmem_limit_bytes=56 * 2**20
        ),
    )(
        bands, block_slot, tile_counties, county_place, label,
        w_first, taps, w_second.T, w_third, w_head.reshape(1, -1),
    )
    return mean, out.reshape(-1)[:grads]


def solution(mesh):
    in_specs = (
        P("state", None, "tile"),
        P("state", "tile"),
        P("state", "tile"),
        P("state", None),
        P("state", "tile"),
        P(),
        P(),
        P(),
        P(),
        P(),
    )
    return jax.shard_map(
        functools.partial(on_device, mesh.shape["tile"], mesh.shape["state"]),
        mesh=mesh,
        in_specs=in_specs,
        out_specs=(P("state", "tile"), P()),
        check_vma=False,
    )
```
